256 devices in a mesh: tea: 8 (over z), stu: 16 (over y, x), hid: 2 (over core).
Axes of the slice: x: 4, y: 4, z: 8, core: 2. Of those that a mesh axis runs over, the one named last changes fastest.
Arguments:
- teacher_hidden: bfloat16 [16384, 8192], P('tea', 'hid'), may hold values from -60 to 60
- projection: bfloat16 [4096, 8192], P('stu', 'hid'), may hold values from -7 to 7
- student_hidden: bfloat16 [10240, 4096], P('stu'), may hold values from -600 to 600
- teacher_segment: int32 [16384], P(('tea', 'hid')), may hold values from 0 to 15, never falling along the last dimension, each value on 1 to 2048 neighbouring positions
- student_segment: int32 [10240], P('stu'), may hold values from 0 to 15, never falling along the last dimension, each value on 1 to 1280 neighbouring positions
Outputs:
- plan: bfloat16 [16384, 10240], P(('tea', 'hid'), 'stu')
- row_pot: float32 [16384], P(('tea', 'hid'))
- col_pot: float32 [10240], P('stu')
The draws below stay inside these ranges and needn't reach their ends.
Inputs may be any that keep to these rules, and one draw needn't show every extreme that they name: `teacher_segment`: never falls along the tokens, and every number of 0 to 15 appears. `student_segment`: never falls along the tokens, and every number of 0 to 15 appears.
All inputs are finite; a program needn't handle non-finite values.
Results may differ from the reference program's by a relative error of at most 0.0073.
Values may be sent and summed in bfloat16 or wider, within the bound.
A program may use at most 192 MiB of HBM per device.

```python
import math
import jax
import jax.numpy as jnp
import numpy as np
from jax import lax

DT = 8192
DS = 4096
ITERS = 3
NSEG = 16
TT = 16384
TS = 10240


def log_scales(key, shape):
    return jnp.exp(jax.random.uniform(key, shape, jnp.float32, 0.0, math.log(10.0)))


def draw_teacher_hidden(key, part):
    key = jax.random.fold_in(key, 11)
    noise_key, scale_key = jax.random.split(key, 2)
    values = jnp.clip(jax.random.normal(noise_key, (TT, DT), jnp.float32), -6.0, 6.0)
    return (values * log_scales(scale_key, (TT, 1))).astype(jnp.bfloat16)


def draw_student_hidden(key, part):
    key = jax.random.fold_in(key, 12)
    noise_key, row_key, col_key = jax.random.split(key, 3)
    noise = jnp.clip(jax.random.normal(noise_key, (TS, DS), jnp.float32), -6.0, 6.0)
    values = noise * log_scales(col_key, (1, DS))
    return (values * log_scales(row_key, (TS, 1))).astype(jnp.bfloat16)


def draw_projection(key, part):
    key = jax.random.fold_in(key, 13)
    values = jnp.clip(jax.random.normal(key, (DS, DT), jnp.float32), -6.0, 6.0) * DT ** (-0.5)
    return values.astype(jnp.bfloat16)


def profile(number_of, total, limit, skew):
    portions = [(1 << 20) // math.isqrt(standing ** skew) + 1 for standing in range(2, number_of + 1)]
    rest, given = total - limit - (number_of - 1), [1] * (number_of - 1)
    while rest > 0:
        free = [i for i in range(number_of - 1) if given[i] < limit]
        whole, left = sum([portions[i] for i in free]), rest
        for i in free:
            more = min(limit - given[i], max(1, left * portions[i] // whole), rest)
            given[i] = given[i] + more
            rest = rest - more
    return np.array([limit] + given)


def uneven(key, count, total, limit, lean):
    if count == 2:
        one = jax.random.randint(key, (), max(1, total - limit), min(limit, total - 1) + 1)
        return jnp.stack([one, total - one])
    lengths = jnp.asarray(profile(count, total, limit, lean), jnp.int32)
    twos = (count - 1) // 2
    source_of, sink = lengths[1:1 + 2 * twos:2], lengths[2:2 + 2 * twos:2]
    room = jnp.minimum(source_of - 1, limit - sink)
    passed = jax.random.randint(jax.random.fold_in(key, 1), (twos,), 0, 1 << 20) % (room + 1)
    lengths = lengths.at[1:1 + 2 * twos:2].set(source_of - passed).at[2:2 + 2 * twos:2].set(sink + passed)
    return lengths[jax.random.permutation(jax.random.fold_in(key, 2), count)]


def setup_inputs(seed: int = 0) -> dict:
    key_list = jax.random.split(jax.random.key(seed), 6)
    teacher_hidden = draw_teacher_hidden(jax.random.fold_in(key_list[5], 71), 0)
    projection = draw_projection(jax.random.fold_in(key_list[5], 71), 0)
    student_hidden = draw_student_hidden(jax.random.fold_in(key_list[5], 71), 0)
    teacher_segment = jnp.searchsorted(jnp.cumsum(uneven(key_list[3], NSEG, TT, 2 * TT // NSEG, 2)), jnp.arange(TT), side="right").astype(jnp.int32)
    student_segment = jnp.searchsorted(jnp.cumsum(uneven(key_list[4], NSEG, TS, 2 * TS // NSEG, 2)), jnp.arange(TS), side="right").astype(jnp.int32)
    return {"teacher_hidden": teacher_hidden, "projection": projection, "student_hidden": student_hidden, "teacher_segment": teacher_segment, "student_segment": student_segment}


EPSILON = 0.004
FLOOR = -1e+30

def masked_lse(values, support, axis):
    top = lax.optimization_barrier(jnp.max(jnp.where(support, values, FLOOR), axis=axis, keepdims=True))
    terms = jnp.where(support, jnp.exp(jnp.where(support, values, top) - top), 0.0)
    return jnp.squeeze(top, axis) + jnp.log(lax.optimization_barrier(jnp.sum(terms, axis=axis)))

def reference(teacher_hidden, projection, student_hidden, teacher_segment, student_segment):
    projected = jnp.dot(teacher_hidden, projection.T, preferred_element_type=jnp.float32).astype(jnp.bfloat16)
    proj_wide = projected.astype(jnp.float32)
    stud_wide = student_hidden.astype(jnp.float32)
    teacher_inv = lax.rsqrt(lax.optimization_barrier(jnp.sum(proj_wide * proj_wide, axis=1)) + 1e-06)
    student_inv = lax.rsqrt(lax.optimization_barrier(jnp.sum(stud_wide * stud_wide, axis=1)) + 1e-06)
    dots = jnp.dot(projected, student_hidden.T, preferred_element_type=jnp.float32)
    scaled = (dots * teacher_inv[:, None] * student_inv[None, :] - 1.0) / EPSILON
    support = teacher_segment[:, None] == student_segment[None, :]
    row_log = jnp.log(lax.optimization_barrier(jnp.sum(support, axis=1)).astype(jnp.float32))
    col_log = jnp.log(lax.optimization_barrier(jnp.sum(support, axis=0)).astype(jnp.float32))
    row_pot = jnp.zeros((TT,), jnp.float32)
    col_pot = jnp.zeros((TS,), jnp.float32)
    for step in range(ITERS):
        row_pot = row_log - masked_lse(scaled + col_pot[None, :], support, 1)
        col_pot = col_log - masked_lse(scaled + row_pot[:, None], support, 0)
    plan = jnp.where(support, jnp.exp(scaled + row_pot[:, None] + col_pot[None, :]), 0.0)
    return (plan.astype(jnp.bfloat16), row_pot, col_pot)
```

```python
import functools

import jax
import jax.numpy as jnp
import numpy as np
from jax import lax
from jax.experimental import pallas as pl
from jax.experimental.pallas import tpu as pltpu
from jax.sharding import PartitionSpec as P

ITERS = 3
INV_EPSILON = float(np.float32(1.0) / np.float32(0.004))
FLOOR = -1e30
SAFE = -1e29
LANES = 128
ROW_BLOCK = 128
CHUNKS = 4
RING = 4
CONTRACT_LAST = (((1,), (1,)), ((), ()))


def to_lanes(part, combine):
    return combine(jnp.transpose(part), axis=0, keepdims=True)


def to_rows(vector):
    count = vector.shape[1]
    return jnp.transpose(jnp.broadcast_to(vector, (LANES, count)))


def merge(slots, width):
    tops, sums, counts = (slots[:, :, k * width:(k + 1) * width] for k in range(3))
    top = jnp.max(tops, axis=0)
    total = jnp.sum(sums * jnp.exp(tops - top), axis=0)
    return top, total, jnp.sum(counts, axis=0)


def kernel(
    peers,
    teacher_ref, proj_ref, student_ref, tseg_ref, sseg_ref,
    plan_ref, row_out, col_out,
    teacher, proj, student, theirs, mine, incoming, gathered, squares, highest, sinv,
    scaled, left, right, spare, row_first, row_next, col_first, col_next,
    teacher_sem, weight_sem, core_send, core_recv, ring_send, ring_recv, send_sem, recv_sem,
):
    rows, cols = scaled.shape
    feats = proj.shape[0]
    chunk = rows // CHUNKS
    half = chunk // 2
    blocks = rows // ROW_BLOCK
    strips = [slice(k * LANES, (k + 1) * LANES) for k in range(cols // LANES)]
    cores = 2
    stu = lax.axis_index("stu")
    hid = lax.axis_index("hid")
    place = lax.axis_index("tea") * cores + hid

    y, x = stu // RING, lax.rem(stu, RING)
    major, minor = y + hid * (x - y), x + hid * (y - x)

    def stu_of(big, small):
        return (big + hid * (small - big)) * RING + small + hid * (big - small)

    def around(index, step):
        return lax.rem(index + step + RING, RING)

    def stu_peer(step):
        return {"stu": lax.rem(stu + step, peers)}

    def tea_peer(step):
        other = lax.rem(place + step, peers)
        return {"tea": other // cores, "hid": lax.rem(other, cores)}

    def teacher_copy(c, whose):
        start = pl.multiple_of((whose * CHUNKS + c) * chunk, chunk)
        return pltpu.make_async_copy(
            teacher_ref.at[pl.ds(start, chunk)], teacher.at[whose * CHUNKS + c], teacher_sem.at[whose * CHUNKS + c]
        )

    proj_copy = pltpu.make_async_copy(proj_ref, proj, weight_sem.at[0])
    proj_copy.start()

    @pl.loop(0, CHUNKS)
    def _(c):
        teacher_copy(c, 1 - hid).start()
        teacher_copy(c, hid).start()

    @pl.loop(0, peers)
    def _(slot):
        big, small = slot // RING, lax.rem(slot, RING)
        source = pl.multiple_of(stu_of(big, small) * feats, feats)
        target = pl.multiple_of(small * feats, feats)
        pltpu.make_async_copy(
            student_ref.at[:, pl.ds(source, feats)], student.at[big, :, pl.ds(target, feats)], weight_sem.at[1]
        ).start()

    barrier = pltpu.get_barrier_semaphore()

    @pl.loop(1, peers)
    def _(step):
        pl.semaphore_signal(barrier, inc=1, device_id=stu_peer(step))
        pl.semaphore_signal(barrier, inc=1, device_id=tea_peer(step))

    left[...] = to_rows(tseg_ref[...].astype(jnp.float32))
    proj_copy.wait()
    pl.semaphore_wait(barrier, 2 * (peers - 1))

    def project(c, whose):
        teacher_copy(c, whose).wait()
        return lax.dot_general(
            teacher[whose * CHUNKS + c], proj[...], CONTRACT_LAST, preferred_element_type=jnp.float32
        )

    def core_copy(c):
        return pltpu.make_async_remote_copy(
            src_ref=theirs.at[c], dst_ref=incoming.at[c],
            send_sem=core_send.at[c], recv_sem=core_recv.at[c], device_id={"hid": 1 - hid},
        )

    def ring_copy(c, stage, ref, big, small):
        return pltpu.make_async_remote_copy(
            src_ref=ref, dst_ref=ref,
            send_sem=ring_send.at[c, stage], recv_sem=ring_recv.at[c, stage],
            device_id={"stu": stu_of(around(big, 0), around(small, 0))},
        )

    def block(c, small, part=slice(None)):
        return gathered.at[c, major, part, pl.ds(pl.multiple_of(around(small, 0) * feats, feats), feats)]

    def bundle(c, big, part=slice(None)):
        return gathered.at[c, around(big, 0), part]

    low, high = pl.ds(0, half), pl.ds(half, half)

    def sends(c, k):
        return [
            lambda: ring_copy(c, 0, block(c, minor), major, minor + 1),
            lambda: ring_copy(c, 1, block(c, minor), major, minor - 1),
            lambda: ring_copy(c, 2, block(c, minor - 1, low), major, minor + 1),
            lambda: ring_copy(c, 3, block(c, minor + 1, high), major, minor - 1),
            lambda: ring_copy(c, 4, bundle(c, major), major + 1, minor),
            lambda: ring_copy(c, 5, bundle(c, major), major - 1, minor),
            lambda: ring_copy(c, 6, bundle(c, major - 1, low), major + 1, minor),
            lambda: ring_copy(c, 7, bundle(c, major + 1, high), major - 1, minor),
        ][k]()

    def arrives(c, k):
        return [
            lambda: ring_copy(c, 0, block(c, minor - 1), major, minor + 1),
            lambda: ring_copy(c, 1, block(c, minor + 1), major, minor - 1),
            lambda: ring_copy(c, 2, block(c, minor + 2, low), major, minor + 1),
            lambda: ring_copy(c, 3, block(c, minor + 2, high), major, minor - 1),
            lambda: ring_copy(c, 4, bundle(c, major - 1), major + 1, minor),
            lambda: ring_copy(c, 5, bundle(c, major + 1), major - 1, minor),
            lambda: ring_copy(c, 6, bundle(c, major + 2, low), major + 1, minor),
            lambda: ring_copy(c, 7, bundle(c, major + 2, high), major - 1, minor),
        ][k]()

    def by_block(body, init=None, first=0, count=blocks):
        def step(b, carry):
            return body(pl.ds(pl.multiple_of(b * ROW_BLOCK, ROW_BLOCK), ROW_BLOCK), carry)
        return lax.fori_loop(first, first + count, step, init)

    def student_norms():
        pltpu.make_async_copy(student, student, weight_sem.at[1]).wait()

        @pl.loop(0, cols // LANES)
        def _(k):
            at = pl.ds(pl.multiple_of(k * LANES, LANES), LANES)
            def add(big, total):
                for j in range(RING * feats // LANES):
                    value = student[big, at, j * LANES:(j + 1) * LANES].astype(jnp.float32)
                    total += value * value
                return total
            total = lax.fori_loop(0, RING, add, jnp.zeros((LANES, LANES), jnp.float32))
            sinv[:, at] = lax.rsqrt(to_lanes(total, jnp.sum) + 1e-06)

    def first_rows(at, carry):
        tinv = lax.rsqrt(jnp.sum(squares[at, :], axis=1, keepdims=True) + 1e-06)
        tseg = left[at, :]
        tops = jnp.full((ROW_BLOCK, LANES), SAFE, jnp.float32)
        count = jnp.zeros((ROW_BLOCK, LANES), jnp.float32)
        for strip in strips:
            support = tseg == sseg_ref[:, strip].astype(jnp.float32)
            value = (scaled[at, strip] * tinv * sinv[:, strip] - 1.0) * INV_EPSILON
            value = jnp.where(support, value, FLOOR)
            scaled[at, strip] = value
            tops = jnp.maximum(tops, value)
            count += jnp.where(support, 1.0, 0.0)
        top = jnp.max(tops, axis=1, keepdims=True)
        total = jnp.zeros((ROW_BLOCK, LANES), jnp.float32)
        for strip in strips:
            total += jnp.exp(scaled[at, strip] - top)
        highest[at, :] = jnp.broadcast_to(top, (ROW_BLOCK, LANES))
        right[at, :] = total
        spare[at, :] = count
        return carry

    def multiply(c):
        at = pl.ds(pl.multiple_of(c * chunk, chunk), chunk)
        scaled[at, :] = jnp.zeros((chunk, cols), jnp.float32)
        squares[at, :] = jnp.zeros((chunk, LANES), jnp.float32)

        @pl.loop(0, RING)
        def _(big):
            scaled[at, :] += lax.dot_general(
                gathered[c, big], student[big], CONTRACT_LAST, preferred_element_type=jnp.float32
            )
            total = squares[at, :]
            for j in range(RING * feats // LANES):
                value = gathered[c, big, :, j * LANES:(j + 1) * LANES].astype(jnp.float32)
                total += value * value
            squares[at, :] = total

        by_block(first_rows, None, c * (chunk // ROW_BLOCK), chunk // ROW_BLOCK)

    @pl.loop(0, CHUNKS + 5)
    def _(slot):
        def due(stage):
            return (slot >= stage) & (slot < CHUNKS + stage)

        @pl.when(due(0))
        def _():
            theirs[slot] = project(slot, 1 - hid)
            core_copy(slot).start()

        @pl.when(due(1))
        def _():
            c = slot - 1
            core_copy(c).wait_recv()
            block(c, minor)[...] = (mine[lax.rem(c, 2)] + incoming[c]).astype(jnp.bfloat16)
            sends(c, 0).start()
            sends(c, 1).start()

        @pl.when(due(0))
        def _():
            mine[lax.rem(slot, 2)] = project(slot, hid)

        for stage in (2, 3, 4, 5):
            @pl.when(due(stage))
            def _():
                c = slot - stage
                near, far = 2 * stage - 4, 2 * stage - 3
                arrives(c, near).wait_recv()
                if stage in (2, 4):
                    sends(c, near + 2).start()
                arrives(c, far).wait_recv()
                if stage == 3:
                    sends(c, near + 2).start()
                if stage < 5:
                    sends(c, far + 2).start()
                else:
                    multiply(c)

        @pl.when(slot == CHUNKS - 1)
        def _():
            student_norms()

    @pl.loop(0, CHUNKS)
    def _(c):
        core_copy(c).wait_send()
        for k in range(8):
            sends(c, k).wait_send()

    def exchange(slots, own, peer, phase):
        @pl.loop(1, peers)
        def _(step):
            pltpu.make_async_remote_copy(
                src_ref=slots.at[own], dst_ref=slots.at[own],
                send_sem=send_sem.at[phase], recv_sem=recv_sem.at[phase],
                device_id=peer(step),
            ).start()

        whole = slots.at[pl.ds(0, peers - 1)]
        done = pltpu.make_async_remote_copy(
            src_ref=whole, dst_ref=whole,
            send_sem=send_sem.at[phase], recv_sem=recv_sem.at[phase],
            device_id=peer(1),
        )
        done.wait_recv()
        done.wait_send()

    row_first[stu] = jnp.concatenate(
        [to_lanes(highest[...], jnp.max), to_lanes(right[...], jnp.sum), to_lanes(spare[...], jnp.sum)],
        axis=1,
    )
    exchange(row_first, stu, stu_peer, 0)
    top, total, row_count = merge(row_first[...], rows)
    row_log = jnp.log(row_count)
    row_pot = row_log - (top + jnp.log(total))
    left[...] = to_rows(row_pot)

    def largest(at, tops):
        pot = left[at, :]
        new = []
        for strip, top in zip(strips, tops):
            value = scaled[at, strip] + pot
            scaled[at, strip] = value
            new.append(jnp.maximum(top, jnp.max(value.reshape(-1, 8, LANES), axis=0)))
        return new

    tops = by_block(largest, [jnp.full((8, LANES), SAFE, jnp.float32) for _ in strips])
    col_top = [jnp.max(top, axis=0, keepdims=True) for top in tops]

    def first_cols(at, carry):
        new = []
        for strip, top, (total, count) in zip(strips, col_top, carry):
            value = scaled[at, strip]
            term = jnp.exp(value - top)
            scaled[at, strip] = term
            total = total + jnp.sum(term.reshape(-1, 8, LANES), axis=0)
            member = jnp.where(value > SAFE, 1.0, 0.0)
            count = count + jnp.sum(member.reshape(-1, 8, LANES), axis=0)
            new.append((total, count))
        return new

    blank = jnp.zeros((8, LANES), jnp.float32)
    sums = by_block(first_cols, [(blank, blank) for _ in strips])
    total = [jnp.sum(total, axis=0, keepdims=True) for total, _ in sums]
    count = [jnp.sum(count, axis=0, keepdims=True) for _, count in sums]
    local_top = jnp.concatenate(col_top, axis=1)
    col_first[place] = jnp.concatenate(col_top + total + count, axis=1)
    exchange(col_first, place, tea_peer, 1)
    top, total, col_count = merge(col_first[...], cols)
    col_log = jnp.log(col_count)
    col_pot = col_log - (top + jnp.log(total))
    gain = jnp.exp(local_top + col_pot)
    first_pot = row_pot

    for step in range(1, ITERS):
        gains = [gain[:, strip] for strip in strips]

        def later_rows(at, carry):
            total = scaled[at, strips[0]] * gains[0]
            for strip, factor in zip(strips[1:], gains[1:]):
                total += scaled[at, strip] * factor
            right[at, :] = total
            return carry

        by_block(later_rows)
        row_next[step - 1, stu] = to_lanes(right[...], jnp.sum)
        exchange(row_next.at[step - 1], stu, stu_peer, 2 * step)
        total = jnp.sum(row_next[step - 1], axis=0)
        fresh = row_count / total
        row_pot = first_pot + jnp.log(fresh)
        left[...] = to_rows(fresh)

        def later_cols(at, sums):
            factor = left[at, :]
            return [
                total + jnp.sum((scaled[at, strip] * factor).reshape(-1, 8, LANES), axis=0)
                for strip, total in zip(strips, sums)
            ]

        sums = by_block(later_cols, [blank for _ in strips])
        total = jnp.concatenate([jnp.sum(s, axis=0, keepdims=True) for s in sums], axis=1)
        col_next[step - 1, place] = total * gain
        exchange(col_next.at[step - 1], place, tea_peer, 2 * step + 1)
        fresh = col_count / jnp.sum(col_next[step - 1], axis=0)
        col_pot = col_pot + jnp.log(fresh)
        gain = gain * fresh

    gains = [gain[:, strip] for strip in strips]

    def finish(at, carry):
        factor = left[at, :]
        for strip, other in zip(strips, gains):
            plan_ref[at, strip] = (scaled[at, strip] * factor * other).astype(jnp.bfloat16)
        return carry

    by_block(finish)
    row_out[...] = row_pot
    col_out[...] = col_pot


def per_device(peers, teacher_hidden, projection, student_hidden, teacher_segment, student_segment):
    rows, cols, feats = teacher_segment.shape[0], student_segment.shape[0], projection.shape[0]
    depth = teacher_hidden.shape[1]
    chunk = rows // CHUNKS
    vmem = pl.BlockSpec(memory_space=pltpu.VMEM)
    anywhere = pl.BlockSpec(memory_space=pl.ANY)
    plan, row_pot, col_pot = pl.pallas_call(
        functools.partial(kernel, peers),
        out_shape=(
            jax.ShapeDtypeStruct((rows, cols), jnp.bfloat16),
            jax.ShapeDtypeStruct((1, rows), jnp.float32),
            jax.ShapeDtypeStruct((1, cols), jnp.float32),
        ),
        in_specs=[anywhere] * 3 + [vmem] * 2,
        out_specs=(vmem, vmem, vmem),
        scratch_shapes=[
            pltpu.VMEM((2 * CHUNKS, chunk, depth), jnp.bfloat16),
            pltpu.VMEM((feats, depth), jnp.bfloat16),
            pltpu.VMEM((RING, cols, RING * feats), jnp.bfloat16),
            pltpu.VMEM((CHUNKS, chunk, feats), jnp.float32),
            pltpu.VMEM((2, chunk, feats), jnp.float32),
            pltpu.VMEM((CHUNKS, chunk, feats), jnp.float32),
            pltpu.VMEM((CHUNKS, RING, chunk, RING * feats), jnp.bfloat16),
            pltpu.VMEM((rows, LANES), jnp.float32),
            pltpu.VMEM((rows, LANES), jnp.float32),
            pltpu.VMEM((1, cols), jnp.float32),
            pltpu.VMEM((rows, cols), jnp.float32),
            pltpu.VMEM((rows, LANES), jnp.float32),
            pltpu.VMEM((rows, LANES), jnp.float32),
            pltpu.VMEM((rows, LANES), jnp.float32),
            pltpu.VMEM((peers, 1, 3 * rows), jnp.float32),
            pltpu.VMEM((ITERS - 1, peers, 1, rows), jnp.float32),
            pltpu.VMEM((peers, 1, 3 * cols), jnp.float32),
            pltpu.VMEM((ITERS - 1, peers, 1, cols), jnp.float32),
            pltpu.SemaphoreType.DMA((2 * CHUNKS,)),
            pltpu.SemaphoreType.DMA((2,)),
            pltpu.SemaphoreType.DMA((CHUNKS,)),
            pltpu.SemaphoreType.DMA((CHUNKS,)),
            pltpu.SemaphoreType.DMA((CHUNKS, 8)),
            pltpu.SemaphoreType.DMA((CHUNKS, 8)),
            pltpu.SemaphoreType.DMA((2 * ITERS,)),
            pltpu.SemaphoreType.DMA((2 * ITERS,)),
        ],
        compiler_params=pltpu.CompilerParams(
            collective_id=1, has_side_effects=True, vmem_limit_bytes=60 * 1024 * 1024
        ),
    )(teacher_hidden, projection, student_hidden, teacher_segment[None, :], student_segment[None, :])
    return plan, row_pot[0], col_pot[0]


def solution(mesh):
    placed = (P("tea", "hid"), P("stu", "hid"), P("stu", None), P(("tea", "hid")), P("stu"))
    return jax.shard_map(
        functools.partial(per_device, mesh.shape["stu"]),
        mesh=mesh,
        in_specs=placed,
        out_specs=(P(("tea", "hid"), "stu"), P(("tea", "hid")), P("stu")),
        check_vma=False,
    )
```

```python
import functools

import jax
import jax.numpy as jnp
import numpy as np
from jax import lax
from jax.experimental import pallas as pl
from jax.experimental.pallas import tpu as pltpu
from jax.sharding import PartitionSpec as P

ITERS = 3
INV_EPSILON = float(np.float32(1.0) / np.float32(0.004))
FLOOR = -1e30
SAFE = -1e29
LANES = 128
ROW_BLOCK = 128
CHUNKS = 4
RING = 4
REACH = 2
CONTRACT_LAST = (((1,), (1,)), ((), ()))


def to_lanes(part, combine):
    return combine(jnp.transpose(part), axis=0, keepdims=True)


def to_rows(vector):
    count = vector.shape[1]
    return jnp.transpose(jnp.broadcast_to(vector, (LANES, count)))


def merge(slots, width):
    tops, sums, counts = (slots[:, :, k * width:(k + 1) * width] for k in range(3))
    top = jnp.max(tops, axis=0)
    total = jnp.sum(sums * jnp.exp(tops - top), axis=0)
    count = jnp.sum(counts, axis=0)
    return jnp.log(count) - (top + jnp.log(total)), count


def kernel(
    peers,
    teacher_ref, proj_ref, student_ref, tseg_ref, sseg_ref,
    plan_ref, row_out, col_out,
    teacher, proj, student, theirs, mine, incoming, gathered, squares, highest, sinv,
    scaled, left, right, spare, gains, row_pots, row_first, row_next, row_last, col_first, col_next, col_last,
    teacher_sem, weight_sem, core_send, core_recv, ring_send, ring_recv, near_send, near_recv, far_send, far_recv,
):
    rows, cols = scaled.shape
    feats = proj.shape[0]
    chunk = rows // CHUNKS
    half = chunk // 2
    blocks = rows // ROW_BLOCK
    strips = [slice(k * LANES, (k + 1) * LANES) for k in range(cols // LANES)]
    cores = 2
    stu = lax.axis_index("stu")
    hid = lax.axis_index("hid")
    place = lax.axis_index("tea") * cores + hid

    y, x = stu // RING, lax.rem(stu, RING)
    major, minor = y + hid * (x - y), x + hid * (y - x)

    def stu_of(big, small):
        return (big + hid * (small - big)) * RING + small + hid * (big - small)

    def around(index, step):
        return lax.rem(index + step + RING, RING)

    def stu_peer(step):
        return {"stu": lax.rem(stu + step + peers, peers)}

    def tea_peer(step):
        other = lax.rem(place + step + peers, peers)
        return {"tea": other // cores, "hid": lax.rem(other, cores)}

    def teacher_copy(c, whose):
        start = pl.multiple_of((whose * CHUNKS + c) * chunk, chunk)
        return pltpu.make_async_copy(
            teacher_ref.at[pl.ds(start, chunk)], teacher.at[whose * CHUNKS + c], teacher_sem.at[whose * CHUNKS + c]
        )

    proj_copy = pltpu.make_async_copy(proj_ref, proj, weight_sem.at[0])
    proj_copy.start()

    @pl.loop(0, CHUNKS)
    def _(c):
        teacher_copy(c, 1 - hid).start()
        teacher_copy(c, hid).start()

    @pl.loop(0, peers)
    def _(slot):
        big, small = slot // RING, lax.rem(slot, RING)
        source = pl.multiple_of(stu_of(big, small) * feats, feats)
        target = pl.multiple_of(small * feats, feats)
        pltpu.make_async_copy(
            student_ref.at[:, pl.ds(source, feats)], student.at[big, :, pl.ds(target, feats)], weight_sem.at[1]
        ).start()

    sseg = sseg_ref[...].reshape(1, cols).astype(jnp.float32)
    barrier = pltpu.get_barrier_semaphore()

    @pl.loop(1, peers)
    def _(step):
        pl.semaphore_signal(barrier, inc=1, device_id=stu_peer(step))
        pl.semaphore_signal(barrier, inc=1, device_id=tea_peer(step))

    proj_copy.wait()

    def project(c, whose):
        teacher_copy(c, whose).wait()
        return lax.dot_general(
            teacher[whose * CHUNKS + c], proj[...], CONTRACT_LAST, preferred_element_type=jnp.float32
        )

    def core_copy(c):
        return pltpu.make_async_remote_copy(
            src_ref=theirs.at[c], dst_ref=incoming.at[c],
            send_sem=core_send.at[c], recv_sem=core_recv.at[c], device_id={"hid": 1 - hid},
        )

    def ring_copy(c, stage, ref, big, small):
        return pltpu.make_async_remote_copy(
            src_ref=ref, dst_ref=ref,
            send_sem=ring_send.at[c, stage], recv_sem=ring_recv.at[c, stage],
            device_id={"stu": stu_of(around(big, 0), around(small, 0))},
        )

    def block(c, small, part=slice(None)):
        return gathered.at[c, major, part, pl.ds(pl.multiple_of(around(small, 0) * feats, feats), feats)]

    def bundle(c, big, part=slice(None)):
        return gathered.at[c, around(big, 0), part]

    low, high = pl.ds(0, half), pl.ds(half, half)

    def sends(c, k):
        return [
            lambda: ring_copy(c, 0, block(c, minor), major, minor + 1),
            lambda: ring_copy(c, 1, block(c, minor), major, minor - 1),
            lambda: ring_copy(c, 2, block(c, minor - 1, low), major, minor + 1),
            lambda: ring_copy(c, 3, block(c, minor + 1, high), major, minor - 1),
            lambda: ring_copy(c, 4, bundle(c, major), major + 1, minor),
            lambda: ring_copy(c, 5, bundle(c, major), major - 1, minor),
            lambda: ring_copy(c, 6, bundle(c, major - 1, low), major + 1, minor),
            lambda: ring_copy(c, 7, bundle(c, major + 1, high), major - 1, minor),
        ][k]()

    def arrives(c, k):
        return [
            lambda: ring_copy(c, 0, block(c, minor - 1), major, minor + 1),
            lambda: ring_copy(c, 1, block(c, minor + 1), major, minor - 1),
            lambda: ring_copy(c, 2, block(c, minor + 2, low), major, minor + 1),
            lambda: ring_copy(c, 3, block(c, minor + 2, high), major, minor - 1),
            lambda: ring_copy(c, 4, bundle(c, major - 1), major + 1, minor),
            lambda: ring_copy(c, 5, bundle(c, major + 1), major - 1, minor),
            lambda: ring_copy(c, 6, bundle(c, major + 2, low), major + 1, minor),
            lambda: ring_copy(c, 7, bundle(c, major + 2, high), major - 1, minor),
        ][k]()

    def by_block(body, init=None, first=0, count=blocks):
        def step(b, carry):
            return body(pl.ds(pl.multiple_of(b * ROW_BLOCK, ROW_BLOCK), ROW_BLOCK), carry)
        return lax.fori_loop(first, first + count, step, init)

    def student_norms():
        pltpu.make_async_copy(student, student, weight_sem.at[1]).wait()

        @pl.loop(0, cols // LANES)
        def _(k):
            at = pl.ds(pl.multiple_of(k * LANES, LANES), LANES)
            def add(big, total):
                for j in range(RING * feats // LANES):
                    value = student[big, at, j * LANES:(j + 1) * LANES].astype(jnp.float32)
                    total += value * value
                return total
            total = lax.fori_loop(0, RING, add, jnp.zeros((LANES, LANES), jnp.float32))
            sinv[:, at] = lax.rsqrt(to_lanes(total, jnp.sum) + 1e-06)

    def first_rows(at, carry):
        tinv = lax.rsqrt(jnp.sum(squares[at, :], axis=1, keepdims=True) + 1e-06)
        tseg = left[at, :]
        tops = jnp.full((ROW_BLOCK, LANES), SAFE, jnp.float32)
        count = jnp.zeros((ROW_BLOCK, LANES), jnp.float32)
        for strip in strips:
            support = tseg == sseg[:, strip]
            value = (scaled[at, strip] * tinv * sinv[:, strip] - 1.0) * INV_EPSILON
            value = jnp.where(support, value, FLOOR)
            scaled[at, strip] = value
            tops = jnp.maximum(tops, value)
            count += jnp.where(support, 1.0, 0.0)
        top = jnp.max(tops, axis=1, keepdims=True)
        total = jnp.zeros((ROW_BLOCK, LANES), jnp.float32)
        for strip in strips:
            total += jnp.exp(scaled[at, strip] - top)
        highest[at, :] = jnp.broadcast_to(top, (ROW_BLOCK, LANES))
        right[at, :] = total
        spare[at, :] = count
        return carry

    def rows_of(c):
        return pl.ds(pl.multiple_of(c * chunk, chunk), chunk)

    def product(c, big):
        return lax.dot_general(
            gathered[c, big], student[big], CONTRACT_LAST, preferred_element_type=jnp.float32
        )

    def squared(c, big, total):
        for j in range(RING * feats // LANES):
            value = gathered[c, big, :, j * LANES:(j + 1) * LANES].astype(jnp.float32)
            total += value * value
        return total

    @pl.loop(0, CHUNKS + 4)
    def _(slot):
        def due(stage):
            return (slot >= stage) & (slot < CHUNKS + stage)

        @pl.when(due(0))
        def _():
            theirs[slot] = project(slot, 1 - hid)

        @pl.when(slot == 0)
        def _():
            left[...] = to_rows(tseg_ref[...].reshape(1, rows).astype(jnp.float32))
            pl.semaphore_wait(barrier, 2 * (peers - 1))

        @pl.when(due(0))
        def _():
            core_copy(slot).start()

        @pl.when(due(1))
        def _():
            c = slot - 1
            core_copy(c).wait_recv()
            block(c, minor)[...] = (mine[lax.rem(c, 2)] + incoming[c]).astype(jnp.bfloat16)
            sends(c, 0).start()
            sends(c, 1).start()

        @pl.when(due(0))
        def _():
            mine[lax.rem(slot, 2)] = project(slot, hid)

        @pl.when(due(3))
        def _():
            c = slot - 3
            arrives(c, 0).wait_recv()
            sends(c, 2).start()
            arrives(c, 1).wait_recv()
            sends(c, 3).start()

        @pl.when(due(4))
        def _():
            c = slot - 4
            arrives(c, 2).wait_recv()
            arrives(c, 3).wait_recv()
            sends(c, 4).start()
            sends(c, 5).start()

    student_norms()

    @pl.loop(0, CHUNKS)
    def _(c):
        arrives(c, 4).wait_recv()
        sends(c, 6).start()
        arrives(c, 5).wait_recv()
        sends(c, 7).start()
        at = rows_of(c)
        before, after = around(major, -1), around(major, 1)
        scaled[at, :] = product(c, major) + product(c, before) + product(c, after)
        total = squared(c, major, jnp.zeros((chunk, LANES), jnp.float32))
        squares[at, :] = squared(c, after, squared(c, before, total))

    def near_copy(slots, peer, phase, step):
        return pltpu.make_async_remote_copy(
            src_ref=slots.at[REACH], dst_ref=slots.at[REACH - step],
            send_sem=near_send.at[phase], recv_sem=near_recv.at[phase], device_id=peer(step),
        )

    def near_start(slots, peer, phase):
        for step in (-2, -1, 1, 2):
            near_copy(slots, peer, phase, step).start()

    def near_all(slots, peer, phase):
        whole = slots.at[pl.ds(0, 2 * REACH)]
        return pltpu.make_async_remote_copy(
            src_ref=whole, dst_ref=whole,
            send_sem=near_send.at[phase], recv_sem=near_recv.at[phase], device_id=peer(1),
        )

    def spread_copy(ref, peer, phase, step):
        return pltpu.make_async_remote_copy(
            src_ref=ref, dst_ref=ref, send_sem=far_send.at[phase], recv_sem=far_recv.at[phase], device_id=peer(step)
        )

    def spread_start(slots, own, peer, phase):
        @pl.loop(1, peers)
        def _(step):
            spread_copy(slots.at[own], peer, phase, step).start()

    def spread_all(slots, peer, phase):
        return spread_copy(slots.at[pl.ds(0, peers - 1)], peer, phase, 1)

    def row_phase(step, c):
        return step * CHUNKS + c

    def col_phase(step):
        return ITERS * CHUNKS + step

    def fold(values):
        return jnp.sum(values.reshape(-1, 8, LANES), axis=0)

    def block_of(c, init, body):
        return by_block(body, init, c * (chunk // ROW_BLOCK), chunk // ROW_BLOCK)

    blank = jnp.zeros((8, LANES), jnp.float32)
    lowest = jnp.full((8, LANES), SAFE, jnp.float32)

    def complete(c):
        arrives(c, 6).wait_recv()
        arrives(c, 7).wait_recv()
        at = rows_of(c)
        opposite = around(major, 2)
        scaled[at, :] += product(c, opposite)
        squares[at, :] = squared(c, opposite, squares[at, :])
        block_of(c, None, first_rows)
        row_first[c, REACH] = jnp.concatenate(
            [
                to_lanes(highest[at, :], jnp.max),
                to_lanes(right[at, :], jnp.sum),
                to_lanes(spare[at, :], jnp.sum),
            ],
            axis=1,
        )
        near_start(row_first.at[c], stu_peer, row_phase(0, c))

    def held_rows(c):
        return row_first[c, REACH, :, 2 * chunk:] > 0.0

    def first_columns(c):
        near_all(row_first.at[c], stu_peer, row_phase(0, c)).wait_recv()
        pot, count = merge(row_first[c], chunk)
        pot = jnp.where(held_rows(c), pot, 0.0)
        row_pots[c] = jnp.concatenate([pot, count], axis=1)
        left[rows_of(c), :] = to_rows(pot)

        def largest(at, tops):
            pot = left[at, :]
            new = []
            for strip, top in zip(strips, tops):
                value = scaled[at, strip] + pot
                scaled[at, strip] = value
                new.append(jnp.maximum(top, jnp.max(value.reshape(-1, 8, LANES), axis=0)))
            return new

        tops = [jnp.max(top, axis=0, keepdims=True) for top in block_of(c, [lowest] * len(strips), largest)]

        def terms(at, carry):
            new = []
            for strip, top, (total, count) in zip(strips, tops, carry):
                value = scaled[at, strip]
                term = jnp.exp(value - top)
                scaled[at, strip] = term
                new.append((total + fold(term), count + fold(jnp.where(value > SAFE, 1.0, 0.0))))
            return new

        sums = block_of(c, [(blank, blank)] * len(strips), terms)
        flat = [jnp.sum(value, axis=0, keepdims=True) for k in range(2) for value in [pair[k] for pair in sums]]
        gains[c] = jnp.concatenate(tops + flat, axis=1)

    @pl.loop(0, CHUNKS + 1)
    def _(slot):
        @pl.when(slot < CHUNKS)
        def _():
            complete(slot)

        @pl.when(slot > 0)
        def _():
            first_columns(slot - 1)

    parts = gains[...]
    local_top = jnp.max(parts[:, :, :cols], axis=0)
    local_sum = jnp.sum(parts[:, :, cols:2 * cols] * jnp.exp(parts[:, :, :cols] - local_top), axis=0)
    own_count = jnp.sum(parts[:, :, 2 * cols:], axis=0)
    col_held = own_count > 0.0
    col_first[REACH] = jnp.concatenate([local_top, local_sum, own_count], axis=1)
    near_start(col_first, tea_peer, col_phase(0))
    near_all(col_first, tea_peer, col_phase(0)).wait_recv()
    col_pot, col_count = merge(col_first[...], cols)
    col_pot = jnp.where(col_held, col_pot, 0.0)
    for c in range(CHUNKS):
        gains[c, :, :cols] = jnp.exp(gains[c, :, :cols] + col_pot)

    def later_rows(step, c):
        def body(at, carry):
            total = scaled[at, strips[0]] * gains[c, :, strips[0]]
            for strip in strips[1:]:
                total += scaled[at, strip] * gains[c, :, strip]
            right[at, :] = total
            return carry

        block_of(c, None, body)
        row_next[step - 1, c, REACH] = to_lanes(right[rows_of(c), :], jnp.sum)
        near_start(row_next.at[step - 1, c], stu_peer, row_phase(step, c))

    def later_cols(step, c, total):
        near_all(row_next.at[step - 1, c], stu_peer, row_phase(step, c)).wait_recv()
        factor = row_pots[c, :, chunk:] / jnp.sum(row_next[step - 1, c], axis=0)
        left[rows_of(c), :] = to_rows(jnp.where(held_rows(c), factor, 0.0))

        def body(at, sums):
            factor = left[at, :]
            return [value + fold(scaled[at, strip] * factor) for strip, value in zip(strips, sums)]

        sums = block_of(c, [blank] * len(strips), body)
        own = jnp.concatenate([jnp.sum(value, axis=0, keepdims=True) for value in sums], axis=1)
        return total + own * gains[c, :, :cols]

    for step in range(1, ITERS):
        last = step == ITERS - 1

        @pl.loop(0, CHUNKS)
        def _(c):
            later_rows(step, c)

        if last:
            def flat(pick):
                return jnp.concatenate([pick(c) for c in range(CHUNKS)], axis=1)

            base = flat(lambda c: jnp.where(held_rows(c), -row_pots[c, :, :chunk], SAFE))
            total = flat(lambda c: row_next[step - 1, c, REACH])
            count = flat(lambda c: row_first[c, REACH, :, 2 * chunk:])
            row_last[stu] = jnp.concatenate([base, total, count], axis=1)
            spread_start(row_last, stu, stu_peer, 0)

        total = lax.fori_loop(
            0, CHUNKS, functools.partial(later_cols, step), jnp.zeros((1, cols), jnp.float32)
        )
        col_next[step - 1, REACH] = total
        near_start(col_next.at[step - 1], tea_peer, col_phase(step))
        if last:
            base = jnp.where(col_held, -col_pot, SAFE)
            col_last[place] = jnp.concatenate([base, total, own_count], axis=1)
            spread_start(col_last, place, tea_peer, 1)
        near_all(col_next.at[step - 1], tea_peer, col_phase(step)).wait_recv()
        fresh = jnp.where(col_held, col_count / jnp.sum(col_next[step - 1], axis=0), 1.0)
        col_pot = col_pot + jnp.log(fresh)
        for c in range(CHUNKS):
            gains[c, :, :cols] = gains[c, :, :cols] * fresh

    @pl.loop(0, CHUNKS)
    def _(c):
        def body(at, carry):
            factor = left[at, :]
            for strip in strips:
                plan_ref[at, strip] = (scaled[at, strip] * factor * gains[c, :, strip]).astype(jnp.bfloat16)
            return carry

        block_of(c, None, body)

    spread_all(row_last, stu_peer, 0).wait_recv()
    row_out[...] = merge(row_last[...], rows)[0].reshape(rows)
    spread_all(col_last, tea_peer, 1).wait_recv()
    col_out[...] = merge(col_last[...], cols)[0].reshape(cols)

    spread_all(row_last, stu_peer, 0).wait_send()
    spread_all(col_last, tea_peer, 1).wait_send()
    near_all(col_first, tea_peer, col_phase(0)).wait_send()
    for step in range(1, ITERS):
        near_all(col_next.at[step - 1], tea_peer, col_phase(step)).wait_send()

    @pl.loop(0, CHUNKS)
    def _(c):
        near_all(row_first.at[c], stu_peer, row_phase(0, c)).wait_send()
        for step in range(1, ITERS):
            near_all(row_next.at[step - 1, c], stu_peer, row_phase(step, c)).wait_send()
        core_copy(c).wait_send()
        for k in range(8):
            sends(c, k).wait_send()


def per_device(peers, teacher_hidden, projection, student_hidden, teacher_segment, student_segment):
    rows, cols, feats = teacher_segment.shape[0], student_segment.shape[0], projection.shape[0]
    depth = teacher_hidden.shape[1]
    chunk = rows // CHUNKS
    vmem = pl.BlockSpec(memory_space=pltpu.VMEM)
    anywhere = pl.BlockSpec(memory_space=pl.ANY)
    plan, row_pot, col_pot = pl.pallas_call(
        functools.partial(kernel, peers),
        out_shape=(
            pltpu.VMEM((rows, cols), jnp.bfloat16),
            pltpu.VMEM((rows,), jnp.float32),
            pltpu.VMEM((cols,), jnp.float32),
        ),
        in_specs=[anywhere] * 3 + [vmem] * 2,
        out_specs=(vmem, vmem, vmem),
        scratch_shapes=[
            pltpu.VMEM((2 * CHUNKS, chunk, depth), jnp.bfloat16),
            pltpu.VMEM((feats, depth), jnp.bfloat16),
            pltpu.VMEM((RING, cols, RING * feats), jnp.bfloat16),
            pltpu.VMEM((CHUNKS, chunk, feats), jnp.float32),
            pltpu.VMEM((2, chunk, feats), jnp.float32),
            pltpu.VMEM((CHUNKS, chunk, feats), jnp.float32),
            pltpu.VMEM((CHUNKS, RING, chunk, RING * feats), jnp.bfloat16),
            pltpu.VMEM((rows, LANES), jnp.float32),
            pltpu.VMEM((rows, LANES), jnp.float32),
            pltpu.VMEM((1, cols), jnp.float32),
            pltpu.VMEM((rows, cols), jnp.float32),
            pltpu.VMEM((rows, LANES), jnp.float32),
            pltpu.VMEM((rows, LANES), jnp.float32),
            pltpu.VMEM((rows, LANES), jnp.float32),
            pltpu.VMEM((CHUNKS, 1, 3 * cols), jnp.float32),
            pltpu.VMEM((CHUNKS, 1, 2 * chunk), jnp.float32),
            pltpu.VMEM((CHUNKS, 2 * REACH + 1, 1, 3 * chunk), jnp.float32),
            pltpu.VMEM((ITERS - 1, CHUNKS, 2 * REACH + 1, 1, chunk), jnp.float32),
            pltpu.VMEM((peers, 1, 3 * rows), jnp.float32),
            pltpu.VMEM((2 * REACH + 1, 1, 3 * cols), jnp.float32),
            pltpu.VMEM((ITERS - 1, 2 * REACH + 1, 1, cols), jnp.float32),
            pltpu.VMEM((peers, 1, 3 * cols), jnp.float32),
            pltpu.SemaphoreType.DMA((2 * CHUNKS,)),
            pltpu.SemaphoreType.DMA((2,)),
            pltpu.SemaphoreType.DMA((CHUNKS,)),
            pltpu.SemaphoreType.DMA((CHUNKS,)),
            pltpu.SemaphoreType.DMA((CHUNKS, 8)),
            pltpu.SemaphoreType.DMA((CHUNKS, 8)),
            pltpu.SemaphoreType.DMA((ITERS * (CHUNKS + 1),)),
            pltpu.SemaphoreType.DMA((ITERS * (CHUNKS + 1),)),
            pltpu.SemaphoreType.DMA((2,)),
            pltpu.SemaphoreType.DMA((2,)),
        ],
        compiler_params=pltpu.CompilerParams(
            collective_id=1, has_side_effects=True, vmem_limit_bytes=60 * 1024 * 1024
        ),
    )(teacher_hidden, projection, student_hidden, teacher_segment, student_segment)
    return plan, row_pot, col_pot


def solution(mesh):
    placed = (P("tea", "hid"), P("stu", "hid"), P("stu", None), P(("tea", "hid")), P("stu"))
    return jax.shard_map(
        functools.partial(per_device, mesh.shape["stu"]),
        mesh=mesh,
        in_specs=placed,
        out_specs=(P(("tea", "hid"), "stu"), P(("tea", "hid")), P("stu")),
        check_vma=False,
    )
```

```python
import functools

import jax
import jax.numpy as jnp
import numpy as np
from jax import lax
from jax.experimental import pallas as pl
from jax.experimental.pallas import tpu as pltpu
from jax.sharding import PartitionSpec as P

ITERS = 3
INV_EPSILON = float(np.float32(1.0) / np.float32(0.004))
FLOOR = -1e30
SAFE = -1e29
LANES = 128
ROW_BLOCK = 128
CHUNKS = 4
RING = 4
REACH = 2
CONTRACT_LAST = (((1,), (1,)), ((), ()))


def to_lanes(part, combine):
    return combine(jnp.transpose(part), axis=0, keepdims=True)


def to_rows(vector):
    count = vector.shape[1]
    return jnp.transpose(jnp.broadcast_to(vector, (LANES, count)))


def merge(slots, width):
    tops, sums, counts = (slots[:, :, k * width:(k + 1) * width] for k in range(3))
    top = jnp.max(tops, axis=0)
    total = jnp.sum(sums * jnp.exp(tops - top), axis=0)
    count = jnp.sum(counts, axis=0)
    return jnp.log(count) - (top + jnp.log(total)), count


def kernel(
    peers,
    teacher_ref, proj_ref, student_ref, tseg_ref, sseg_ref,
    plan_ref, row_out, col_out,
    teacher, proj, student, theirs, mine, incoming, gathered, squares, highest, sinv,
    scaled, left, right, spare, gains, row_pots, row_first, row_next, row_last, col_first, col_next, col_last,
    teacher_sem, weight_sem, core_send, core_recv, ring_send, ring_recv, near_send, near_recv, far_send, far_recv,
):
    rows, cols = scaled.shape
    feats = proj.shape[0]
    chunk = rows // CHUNKS
    half = chunk // 2
    blocks = rows // ROW_BLOCK
    strips = [slice(k * LANES, (k + 1) * LANES) for k in range(cols // LANES)]
    cores = 2
    stu = lax.axis_index("stu")
    hid = lax.axis_index("hid")
    place = lax.axis_index("tea") * cores + hid

    y, x = stu // RING, lax.rem(stu, RING)
    major, minor = y + hid * (x - y), x + hid * (y - x)

    def stu_of(big, small):
        return (big + hid * (small - big)) * RING + small + hid * (big - small)

    def around(index, step):
        return lax.rem(index + step + RING, RING)

    def stu_peer(step):
        return {"stu": lax.rem(stu + step + peers, peers)}

    def tea_peer(step):
        other = lax.rem(place + step + peers, peers)
        return {"tea": other // cores, "hid": lax.rem(other, cores)}

    def teacher_copy(c, whose):
        start = pl.multiple_of((whose * CHUNKS + c) * chunk, chunk)
        return pltpu.make_async_copy(
            teacher_ref.at[pl.ds(start, chunk)], teacher.at[whose * CHUNKS + c], teacher_sem.at[whose * CHUNKS + c]
        )

    proj_copy = pltpu.make_async_copy(proj_ref, proj, weight_sem.at[0])
    proj_copy.start()

    @pl.loop(0, CHUNKS)
    def _(c):
        teacher_copy(c, 1 - hid).start()
        teacher_copy(c, hid).start()

    @pl.loop(0, peers)
    def _(slot):
        big, small = slot // RING, lax.rem(slot, RING)
        source = pl.multiple_of(stu_of(big, small) * feats, feats)
        target = pl.multiple_of(small * feats, feats)
        pltpu.make_async_copy(
            student_ref.at[:, pl.ds(source, feats)], student.at[big, :, pl.ds(target, feats)], weight_sem.at[1]
        ).start()

    sseg = sseg_ref[...].reshape(1, cols).astype(jnp.float32)
    barrier = pltpu.get_barrier_semaphore()

    @pl.loop(1, peers)
    def _(step):
        pl.semaphore_signal(barrier, inc=1, device_id=stu_peer(step))
        pl.semaphore_signal(barrier, inc=1, device_id=tea_peer(step))

    proj_copy.wait()

    def project(c, whose):
        teacher_copy(c, whose).wait()
        return lax.dot_general(
            teacher[whose * CHUNKS + c], proj[...], CONTRACT_LAST, preferred_element_type=jnp.float32
        )

    def core_copy(c):
        return pltpu.make_async_remote_copy(
            src_ref=theirs.at[c], dst_ref=incoming.at[c],
            send_sem=core_send.at[c], recv_sem=core_recv.at[c], device_id={"hid": 1 - hid},
        )

    def ring_copy(c, stage, ref, big, small):
        return pltpu.make_async_remote_copy(
            src_ref=ref, dst_ref=ref,
            send_sem=ring_send.at[c, stage], recv_sem=ring_recv.at[c, stage],
            device_id={"stu": stu_of(around(big, 0), around(small, 0))},
        )

    def block(c, small, part=slice(None)):
        return gathered.at[c, major, part, pl.ds(pl.multiple_of(around(small, 0) * feats, feats), feats)]

    def bundle(c, big, part=slice(None)):
        return gathered.at[c, around(big, 0), part]

    low, high = pl.ds(0, half), pl.ds(half, half)

    def sends(c, k):
        return [
            lambda: ring_copy(c, 0, block(c, minor), major, minor + 1),
            lambda: ring_copy(c, 1, block(c, minor), major, minor - 1),
            lambda: ring_copy(c, 2, block(c, minor - 1, low), major, minor + 1),
            lambda: ring_copy(c, 3, block(c, minor + 1, high), major, minor - 1),
            lambda: ring_copy(c, 4, bundle(c, major), major + 1, minor),
            lambda: ring_copy(c, 5, bundle(c, major), major - 1, minor),
            lambda: ring_copy(c, 6, bundle(c, major - 1, low), major + 1, minor),
            lambda: ring_copy(c, 7, bundle(c, major + 1, high), major - 1, minor),
        ][k]()

    def arrives(c, k):
        return [
            lambda: ring_copy(c, 0, block(c, minor - 1), major, minor + 1),
            lambda: ring_copy(c, 1, block(c, minor + 1), major, minor - 1),
            lambda: ring_copy(c, 2, block(c, minor + 2, low), major, minor + 1),
            lambda: ring_copy(c, 3, block(c, minor + 2, high), major, minor - 1),
            lambda: ring_copy(c, 4, bundle(c, major - 1), major + 1, minor),
            lambda: ring_copy(c, 5, bundle(c, major + 1), major - 1, minor),
            lambda: ring_copy(c, 6, bundle(c, major + 2, low), major + 1, minor),
            lambda: ring_copy(c, 7, bundle(c, major + 2, high), major - 1, minor),
        ][k]()

    def by_block(body, init=None, first=0, count=blocks):
        def step(b, carry):
            return body(pl.ds(pl.multiple_of(b * ROW_BLOCK, ROW_BLOCK), ROW_BLOCK), carry)
        return lax.fori_loop(first, first + count, step, init)

    def student_norms():
        pltpu.make_async_copy(student, student, weight_sem.at[1]).wait()

        @pl.loop(0, cols // LANES)
        def _(k):
            at = pl.ds(pl.multiple_of(k * LANES, LANES), LANES)
            def add(big, total):
                for j in range(RING * feats // LANES):
                    value = student[big, at, j * LANES:(j + 1) * LANES].astype(jnp.float32)
                    total += value * value
                return total
            total = lax.fori_loop(0, RING, add, jnp.zeros((LANES, LANES), jnp.float32))
            sinv[:, at] = lax.rsqrt(to_lanes(total, jnp.sum) + 1e-06)

    def first_rows(at, carry):
        tinv = lax.rsqrt(jnp.sum(squares[at, :], axis=1, keepdims=True) + 1e-06)
        tseg = left[at, :]
        tops = jnp.full((ROW_BLOCK, LANES), SAFE, jnp.float32)
        count = jnp.zeros((ROW_BLOCK, LANES), jnp.float32)
        for strip in strips:
            support = tseg == sseg[:, strip]
            value = (scaled[at, strip] * tinv * sinv[:, strip] - 1.0) * INV_EPSILON
            value = jnp.where(support, value, FLOOR)
            scaled[at, strip] = value
            tops = jnp.maximum(tops, value)
            count += jnp.where(support, 1.0, 0.0)
        top = jnp.max(tops, axis=1, keepdims=True)
        total = jnp.zeros((ROW_BLOCK, LANES), jnp.float32)
        for strip in strips:
            total += jnp.exp(scaled[at, strip] - top)
        highest[at, :] = jnp.broadcast_to(top, (ROW_BLOCK, LANES))
        right[at, :] = total
        spare[at, :] = count
        return carry

    def rows_of(c):
        return pl.ds(pl.multiple_of(c * chunk, chunk), chunk)

    def product(c, big):
        return lax.dot_general(
            gathered[c, big], student[big], CONTRACT_LAST, preferred_element_type=jnp.float32
        )

    def squared(c, big, total):
        for j in range(RING * feats // LANES):
            value = gathered[c, big, :, j * LANES:(j + 1) * LANES].astype(jnp.float32)
            total += value * value
        return total

    @pl.loop(0, CHUNKS + 4)
    def _(slot):
        def due(stage):
            return (slot >= stage) & (slot < CHUNKS + stage)

        @pl.when(due(0))
        def _():
            theirs[slot] = project(slot, 1 - hid)

        @pl.when(slot == 0)
        def _():
            left[...] = to_rows(tseg_ref[...].reshape(1, rows).astype(jnp.float32))
            pl.semaphore_wait(barrier, 2 * (peers - 1))

        @pl.when(due(0))
        def _():
            core_copy(slot).start()

        @pl.when(due(1))
        def _():
            c = slot - 1
            core_copy(c).wait_recv()
            block(c, minor)[...] = (mine[lax.rem(c, 2)] + incoming[c]).astype(jnp.bfloat16)
            sends(c, 0).start()
            sends(c, 1).start()

        @pl.when(due(0))
        def _():
            mine[lax.rem(slot, 2)] = project(slot, hid)

        @pl.when(due(3))
        def _():
            c = slot - 3
            arrives(c, 0).wait_recv()
            sends(c, 2).start()
            arrives(c, 1).wait_recv()
            sends(c, 3).start()

        @pl.when(due(4))
        def _():
            c = slot - 4
            arrives(c, 2).wait_recv()
            arrives(c, 3).wait_recv()
            sends(c, 4).start()
            sends(c, 5).start()

    student_norms()

    @pl.loop(0, CHUNKS)
    def _(c):
        arrives(c, 4).wait_recv()
        sends(c, 6).start()
        arrives(c, 5).wait_recv()
        sends(c, 7).start()
        at = rows_of(c)
        before, after = around(major, -1), around(major, 1)
        scaled[at, :] = product(c, major) + product(c, before) + product(c, after)
        total = squared(c, major, jnp.zeros((chunk, LANES), jnp.float32))
        squares[at, :] = squared(c, after, squared(c, before, total))

    def near_copy(slots, peer, phase, step):
        return pltpu.make_async_remote_copy(
            src_ref=slots.at[REACH], dst_ref=slots.at[REACH - step],
            send_sem=near_send.at[phase], recv_sem=near_recv.at[phase], device_id=peer(step),
        )

    def near_start(slots, peer, phase):
        for step in (-2, -1, 1, 2):
            near_copy(slots, peer, phase, step).start()

    def near_all(slots, peer, phase):
        whole = slots.at[pl.ds(0, 2 * REACH)]
        return pltpu.make_async_remote_copy(
            src_ref=whole, dst_ref=whole,
            send_sem=near_send.at[phase], recv_sem=near_recv.at[phase], device_id=peer(1),
        )

    def spread_copy(ref, peer, phase, step, sends=far_send, recvs=far_recv):
        return pltpu.make_async_remote_copy(
            src_ref=ref, dst_ref=ref, send_sem=sends.at[phase], recv_sem=recvs.at[phase], device_id=peer(step)
        )

    def row_phase(step):
        return CHUNKS + step - 1

    def col_phase(step):
        return CHUNKS + ITERS - 1 + step

    def fold(values):
        return jnp.sum(values.reshape(-1, 8, LANES), axis=0)

    def block_of(c, init, body):
        return by_block(body, init, c * (chunk // ROW_BLOCK), chunk // ROW_BLOCK)

    blank = jnp.zeros((8, LANES), jnp.float32)
    lowest = jnp.full((8, LANES), SAFE, jnp.float32)

    def complete(c):
        arrives(c, 6).wait_recv()
        arrives(c, 7).wait_recv()
        at = rows_of(c)
        opposite = around(major, 2)
        scaled[at, :] += product(c, opposite)
        squares[at, :] = squared(c, opposite, squares[at, :])
        block_of(c, None, first_rows)
        row_first[c, REACH] = jnp.concatenate(
            [
                to_lanes(highest[at, :], jnp.max),
                to_lanes(right[at, :], jnp.sum),
                to_lanes(spare[at, :], jnp.sum),
            ],
            axis=1,
        )
        near_start(row_first.at[c], stu_peer, c)

    def held_rows(c):
        return row_first[c, REACH, :, 2 * chunk:] > 0.0

    def first_columns(c):
        near_all(row_first.at[c], stu_peer, c).wait_recv()
        pot, count = merge(row_first[c], chunk)
        pot = jnp.where(held_rows(c), pot, 0.0)
        row_pots[c] = jnp.concatenate([pot, count], axis=1)
        left[rows_of(c), :] = to_rows(pot)

        def largest(at, tops):
            pot = left[at, :]
            new = []
            for strip, top in zip(strips, tops):
                value = scaled[at, strip] + pot
                scaled[at, strip] = value
                new.append(jnp.maximum(top, jnp.max(value.reshape(-1, 8, LANES), axis=0)))
            return new

        tops = [jnp.max(top, axis=0, keepdims=True) for top in block_of(c, [lowest] * len(strips), largest)]

        def terms(at, carry):
            new = []
            for strip, top, (total, count) in zip(strips, tops, carry):
                value = scaled[at, strip]
                term = jnp.exp(value - top)
                scaled[at, strip] = term
                new.append((total + fold(term), count + fold(jnp.where(value > SAFE, 1.0, 0.0))))
            return new

        sums = block_of(c, [(blank, blank)] * len(strips), terms)
        flat = [jnp.sum(value, axis=0, keepdims=True) for k in range(2) for value in [pair[k] for pair in sums]]
        gains[c] = jnp.concatenate(tops + flat, axis=1)

    @pl.loop(0, CHUNKS + 1)
    def _(slot):
        @pl.when(slot < CHUNKS)
        def _():
            complete(slot)

        @pl.when(slot > 0)
        def _():
            first_columns(slot - 1)

    parts = gains[...]
    local_top = jnp.max(parts[:, :, :cols], axis=0)
    local_sum = jnp.sum(parts[:, :, cols:2 * cols] * jnp.exp(parts[:, :, :cols] - local_top), axis=0)
    own_count = jnp.sum(parts[:, :, 2 * cols:], axis=0)
    col_held = own_count > 0.0
    col_first[REACH] = jnp.concatenate([local_top, local_sum, own_count], axis=1)
    near_start(col_first, tea_peer, col_phase(0))

    @pl.loop(0, CHUNKS)
    def _(c):
        near_all(row_first.at[c], stu_peer, c).wait_send()
        core_copy(c).wait_send()
        for k in range(8):
            sends(c, k).wait_send()

    near_all(col_first, tea_peer, col_phase(0)).wait_recv()
    col_pot, col_count = merge(col_first[...], cols)
    col_pot = jnp.where(col_held, col_pot, 0.0)
    for c in range(CHUNKS):
        gains[c, :, :cols] = jnp.exp(gains[c, :, :cols] + col_pot)

    def by_chunk_block(body, init=None):
        def step(b, carry):
            at = pl.ds(pl.multiple_of(b * ROW_BLOCK, ROW_BLOCK), ROW_BLOCK)
            return body(at, gains.at[b // (chunk // ROW_BLOCK)], carry)
        return lax.fori_loop(0, blocks, step, init)

    def across(pick):
        return jnp.concatenate([pick(c) for c in range(CHUNKS)], axis=1)

    row_held = across(held_rows)
    first_pot = across(lambda c: row_pots[c, :, :chunk])
    row_count = across(lambda c: row_pots[c, :, chunk:])

    for step in range(1, ITERS):
        last = step == ITERS - 1
        row_slots, col_slots = row_next.at[step - 1], col_next.at[step - 1]

        def later_rows(at, gain, carry):
            total = scaled[at, strips[0]] * gain[:, strips[0]]
            for strip in strips[1:]:
                total += scaled[at, strip] * gain[:, strip]
            right[at, :] = total
            return carry

        by_chunk_block(later_rows)
        row_slots[REACH] = to_lanes(right[...], jnp.sum)
        near_start(row_slots, stu_peer, row_phase(step))
        near_all(row_slots, stu_peer, row_phase(step)).wait_recv()
        factor = row_count / jnp.sum(row_slots[...], axis=0)
        left[...] = to_rows(jnp.where(row_held, factor, 0.0))

        def later_cols(at, gain, sums):
            factor = left[at, :]
            return [
                value + fold(scaled[at, strip] * factor) * gain[:, strip] for strip, value in zip(strips, sums)
            ]

        sums = by_chunk_block(later_cols, [blank] * len(strips))
        total = jnp.concatenate([jnp.sum(value, axis=0, keepdims=True) for value in sums], axis=1)
        if last:
            base = jnp.where(col_held, -col_pot - jnp.log(col_count), SAFE)
            col_last[place] = jnp.concatenate([base, total], axis=1)
            for k in (-2, -1, 1, 2):
                spread_copy(col_last.at[place], tea_peer, col_phase(step), k, near_send, near_recv).start()

            @pl.loop(REACH + 1, peers - REACH)
            def _(k):
                spread_copy(col_last.at[place], tea_peer, 1, k).start()

            row_last[stu] = jnp.where(row_held, first_pot + jnp.log(factor), FLOOR)

            @pl.loop(1, peers)
            def _(k):
                spread_copy(row_last.at[stu], stu_peer, 0, k).start()

            near_cols = spread_copy(
                col_last.at[pl.ds(0, 2 * REACH)], tea_peer, col_phase(step), 1, near_send, near_recv
            )
            near_cols.wait_recv()
            for k in (-2, -1, 1, 2):
                total += col_last[lax.rem(place + k + peers, peers), :, cols:]
        else:
            col_slots[REACH] = total
            near_start(col_slots, tea_peer, col_phase(step))
            near_all(col_slots, tea_peer, col_phase(step)).wait_recv()
            total = jnp.sum(col_slots[...], axis=0)
        fresh = jnp.where(col_held, col_count / total, 1.0)
        col_pot = col_pot + jnp.log(fresh)
        for c in range(CHUNKS):
            gains[c, :, :cols] = gains[c, :, :cols] * fresh

    def finish(at, gain, carry):
        factor = left[at, :]
        for strip in strips:
            plan_ref[at, strip] = (scaled[at, strip] * factor * gain[:, strip]).astype(jnp.bfloat16)
        return carry

    by_chunk_block(finish)
    far_rows = spread_copy(row_last.at[pl.ds(0, peers - 1)], stu_peer, 0, 1)
    far_cols = spread_copy(col_last.at[pl.ds(0, peers - 1 - 2 * REACH)], tea_peer, 1, 1)
    near_cols.wait_send()
    near_all(col_first, tea_peer, col_phase(0)).wait_send()
    for step in range(1, ITERS):
        near_all(row_next.at[step - 1], stu_peer, row_phase(step)).wait_send()
    for step in range(1, ITERS - 1):
        near_all(col_next.at[step - 1], tea_peer, col_phase(step)).wait_send()
    far_rows.wait_recv()
    row_out[...] = jnp.max(row_last[...], axis=0).reshape(rows)
    far_cols.wait_recv()
    base, total = col_last[:, :, :cols], col_last[:, :, cols:]
    top = jnp.max(base, axis=0)
    col_out[...] = -(top + jnp.log(jnp.sum(total * jnp.exp(base - top), axis=0))).reshape(cols)

    far_rows.wait_send()
    far_cols.wait_send()

def hand_over_kernel(plan_ref, row_ref, col_ref, plan_out, row_out, col_out, sems):
    copies = [
        pltpu.make_async_copy(source, target, sems.at[k])
        for k, (source, target) in enumerate(((plan_ref, plan_out), (row_ref, row_out), (col_ref, col_out)))
    ]
    for copy in copies:
        copy.start()
    for copy in copies:
        copy.wait()


def hand_over(*held):
    anywhere = pl.BlockSpec(memory_space=pl.ANY)
    return pl.pallas_call(
        hand_over_kernel,
        out_shape=tuple(jax.ShapeDtypeStruct(value.shape, value.dtype) for value in held),
        in_specs=[pl.BlockSpec(memory_space=pltpu.VMEM)] * len(held),
        out_specs=(anywhere,) * len(held),
        scratch_shapes=[pltpu.SemaphoreType.DMA((len(held),))],
    )(*(pltpu.with_memory_space_constraint(value, pltpu.VMEM) for value in held))


def per_device(peers, teacher_hidden, projection, student_hidden, teacher_segment, student_segment):
    rows, cols, feats = teacher_segment.shape[0], student_segment.shape[0], projection.shape[0]
    depth = teacher_hidden.shape[1]
    chunk = rows // CHUNKS
    vmem = pl.BlockSpec(memory_space=pltpu.VMEM)
    anywhere = pl.BlockSpec(memory_space=pl.ANY)
    plan, row_pot, col_pot = pl.pallas_call(
        functools.partial(kernel, peers),
        out_shape=(
            pltpu.VMEM((rows, cols), jnp.bfloat16),
            pltpu.VMEM((rows,), jnp.float32),
            pltpu.VMEM((cols,), jnp.float32),
        ),
        in_specs=[anywhere] * 3 + [vmem] * 2,
        out_specs=(vmem, vmem, vmem),
        scratch_shapes=[
            pltpu.VMEM((2 * CHUNKS, chunk, depth), jnp.bfloat16),
            pltpu.VMEM((feats, depth), jnp.bfloat16),
            pltpu.VMEM((RING, cols, RING * feats), jnp.bfloat16),
            pltpu.VMEM((CHUNKS, chunk, feats), jnp.float32),
            pltpu.VMEM((2, chunk, feats), jnp.float32),
            pltpu.VMEM((CHUNKS, chunk, feats), jnp.float32),
            pltpu.VMEM((CHUNKS, RING, chunk, RING * feats), jnp.bfloat16),
            pltpu.VMEM((rows, LANES), jnp.float32),
            pltpu.VMEM((rows, LANES), jnp.float32),
            pltpu.VMEM((1, cols), jnp.float32),
            pltpu.VMEM((rows, cols), jnp.float32),
            pltpu.VMEM((rows, LANES), jnp.float32),
            pltpu.VMEM((rows, LANES), jnp.float32),
            pltpu.VMEM((rows, LANES), jnp.float32),
            pltpu.VMEM((CHUNKS, 1, 3 * cols), jnp.float32),
            pltpu.VMEM((CHUNKS, 1, 2 * chunk), jnp.float32),
            pltpu.VMEM((CHUNKS, 2 * REACH + 1, 1, 3 * chunk), jnp.float32),
            pltpu.VMEM((ITERS - 1, 2 * REACH + 1, 1, rows), jnp.float32),
            pltpu.VMEM((peers, 1, rows), jnp.float32),
            pltpu.VMEM((2 * REACH + 1, 1, 3 * cols), jnp.float32),
            pltpu.VMEM((ITERS - 1, 2 * REACH + 1, 1, cols), jnp.float32),
            pltpu.VMEM((peers, 1, 2 * cols), jnp.float32),
            pltpu.SemaphoreType.DMA((2 * CHUNKS,)),
            pltpu.SemaphoreType.DMA((2,)),
            pltpu.SemaphoreType.DMA((CHUNKS,)),
            pltpu.SemaphoreType.DMA((CHUNKS,)),
            pltpu.SemaphoreType.DMA((CHUNKS, 8)),
            pltpu.SemaphoreType.DMA((CHUNKS, 8)),
            pltpu.SemaphoreType.DMA((CHUNKS + 2 * ITERS - 1,)),
            pltpu.SemaphoreType.DMA((CHUNKS + 2 * ITERS - 1,)),
            pltpu.SemaphoreType.DMA((2,)),
            pltpu.SemaphoreType.DMA((2,)),
        ],
        compiler_params=pltpu.CompilerParams(
            collective_id=1, has_side_effects=True, vmem_limit_bytes=60 * 1024 * 1024
        ),
    )(teacher_hidden, projection, student_hidden, teacher_segment, student_segment)
    return hand_over(plan, row_pot, col_pot)


def solution(mesh):
    placed = (P("tea", "hid"), P("stu", "hid"), P("stu", None), P(("tea", "hid")), P("stu"))
    return jax.shard_map(
        functools.partial(per_device, mesh.shape["stu"]),
        mesh=mesh,
        in_specs=placed,
        out_specs=(P(("tea", "hid"), "stu"), P(("tea", "hid")), P("stu")),
        check_vma=False,
    )
```

```python
import functools

import jax
import jax.numpy as jnp
import numpy as np
from jax import lax
from jax.experimental import pallas as pl
from jax.experimental.pallas import tpu as pltpu
from jax.sharding import PartitionSpec as P

ITERS = 3
INV_EPSILON = float(np.float32(1.0) / np.float32(0.004))
FLOOR = -1e30
SAFE = -1e29
LANES = 128
ROW_BLOCK = 128
CHUNKS = 4
RING = 4
REACH = 2
CONTRACT_LAST = (((1,), (1,)), ((), ()))


def to_lanes(part, combine):
    return combine(jnp.transpose(part), axis=0, keepdims=True)


def to_rows(vector):
    count = vector.shape[1]
    return jnp.transpose(jnp.broadcast_to(vector, (LANES, count)))


def merge(slots, width):
    tops, sums, counts = (slots[:, :, k * width:(k + 1) * width] for k in range(3))
    top = jnp.max(tops, axis=0)
    total = jnp.sum(sums * jnp.exp(tops - top), axis=0)
    count = jnp.sum(counts, axis=0)
    return jnp.log(count) - (top + jnp.log(total)), count


def kernel(
    peers,
    teacher_ref, proj_ref, student_ref, tseg_ref, sseg_ref,
    plan_ref, row_out, col_out,
    teacher, proj, student, theirs, mine, incoming, gathered, squares, highest, sinv,
    scaled, left, right, spare, gains, row_pots, row_first, row_next, row_last, col_first, col_next, col_last,
    teacher_sem, weight_sem, core_send, core_recv, ring_send, ring_recv, near_send, near_recv, far_send, far_recv,
):
    rows, cols = scaled.shape
    feats = proj.shape[0]
    chunk = rows // CHUNKS
    half = chunk // 2
    blocks = rows // ROW_BLOCK
    strips = [slice(k * LANES, (k + 1) * LANES) for k in range(cols // LANES)]
    cores = 2
    stu = lax.axis_index("stu")
    hid = lax.axis_index("hid")
    place = lax.axis_index("tea") * cores + hid

    y, x = stu // RING, lax.rem(stu, RING)
    major, minor = y + hid * (x - y), x + hid * (y - x)

    def stu_of(big, small):
        return (big + hid * (small - big)) * RING + small + hid * (big - small)

    def around(index, step):
        return lax.rem(index + step + RING, RING)

    def stu_peer(step):
        return {"stu": lax.rem(stu + step + peers, peers)}

    def tea_peer(step):
        other = lax.rem(place + step + peers, peers)
        return {"tea": other // cores, "hid": lax.rem(other, cores)}

    def teacher_copy(c, whose):
        start = pl.multiple_of((whose * CHUNKS + c) * chunk, chunk)
        return pltpu.make_async_copy(
            teacher_ref.at[pl.ds(start, chunk)], teacher.at[whose * CHUNKS + c], teacher_sem.at[whose * CHUNKS + c]
        )

    proj_copy = pltpu.make_async_copy(proj_ref, proj, weight_sem.at[0])
    proj_copy.start()

    @pl.loop(0, CHUNKS)
    def _(c):
        teacher_copy(c, 1 - hid).start()
        teacher_copy(c, hid).start()

    @pl.loop(0, peers)
    def _(slot):
        big, small = slot // RING, lax.rem(slot, RING)
        source = pl.multiple_of(stu_of(big, small) * feats, feats)
        target = pl.multiple_of(small * feats, feats)
        pltpu.make_async_copy(
            student_ref.at[:, pl.ds(source, feats)], student.at[big, :, pl.ds(target, feats)], weight_sem.at[1]
        ).start()

    sseg = sseg_ref[...].reshape(1, cols).astype(jnp.float32)
    barrier = pltpu.get_barrier_semaphore()

    @pl.loop(1, peers)
    def _(step):
        pl.semaphore_signal(barrier, inc=1, device_id=stu_peer(step))
        pl.semaphore_signal(barrier, inc=1, device_id=tea_peer(step))

    proj_copy.wait()

    def project(c, whose):
        teacher_copy(c, whose).wait()
        return lax.dot_general(
            teacher[whose * CHUNKS + c], proj[...], CONTRACT_LAST, preferred_element_type=jnp.float32
        )

    def core_copy(c):
        return pltpu.make_async_remote_copy(
            src_ref=theirs.at[c], dst_ref=incoming.at[c],
            send_sem=core_send.at[c], recv_sem=core_recv.at[c], device_id={"hid": 1 - hid},
        )

    def ring_copy(c, stage, ref, big, small):
        return pltpu.make_async_remote_copy(
            src_ref=ref, dst_ref=ref,
            send_sem=ring_send.at[c, stage], recv_sem=ring_recv.at[c, stage],
            device_id={"stu": stu_of(around(big, 0), around(small, 0))},
        )

    def block(c, big, small, part=slice(None)):
        return gathered.at[c, around(big, 0), part, pl.ds(pl.multiple_of(around(small, 0) * feats, feats), feats)]

    def bundle(c, big, part=slice(None)):
        return gathered.at[c, around(big, 0), part]

    low, high = pl.ds(0, half), pl.ds(half, half)
    offsets = (0, -1, 1, 2)

    def along_minor(c, k, side, small, part=slice(None)):
        return ring_copy(c, k, block(c, major, small, part), major, minor + side)

    def along_major(c, which, side, big):
        return ring_copy(
            c, 4 + 2 * which + (side < 0), block(c, big, minor + offsets[which]), major + side, minor
        )

    def relay(c, side, big):
        return ring_copy(c, 12 + (side < 0), bundle(c, big, low if side > 0 else high), major + side, minor)

    def send_major(c, which):
        along_major(c, which, 1, major).start()
        along_major(c, which, -1, major).start()

    def own_stage(c):
        along_minor(c, 0, 1, minor).start()
        along_minor(c, 1, -1, minor).start()
        send_major(c, 0)

    def near_stage(c):
        along_minor(c, 0, 1, minor - 1).wait_recv()
        along_minor(c, 2, 1, minor - 1, low).start()
        send_major(c, 1)
        along_minor(c, 1, -1, minor + 1).wait_recv()
        along_minor(c, 3, -1, minor + 1, high).start()
        send_major(c, 2)

    def far_stage(c):
        along_minor(c, 2, 1, minor + 2, low).wait_recv()
        along_minor(c, 3, -1, minor + 2, high).wait_recv()
        send_major(c, 3)

    def relay_stage(c):
        for side in (1, -1):
            for which in range(4):
                along_major(c, which, side, major - side).wait_recv()
            relay(c, side, major - side).start()

    def last_stage(c):
        relay(c, 1, major + 2).wait_recv()
        relay(c, -1, major + 2).wait_recv()

    def sent(c):
        along_minor(c, 0, 1, minor).wait_send()
        along_minor(c, 1, -1, minor).wait_send()
        along_minor(c, 2, 1, minor - 1, low).wait_send()
        along_minor(c, 3, -1, minor + 1, high).wait_send()
        for side in (1, -1):
            for which in range(4):
                along_major(c, which, side, major).wait_send()
            relay(c, side, major - side).wait_send()

    def by_block(body, init=None, first=0, count=blocks):
        def step(b, carry):
            return body(pl.ds(pl.multiple_of(b * ROW_BLOCK, ROW_BLOCK), ROW_BLOCK), carry)
        return lax.fori_loop(first, first + count, step, init)

    def student_norms():
        pltpu.make_async_copy(student, student, weight_sem.at[1]).wait()

        @pl.loop(0, cols // LANES)
        def _(k):
            at = pl.ds(pl.multiple_of(k * LANES, LANES), LANES)
            def add(big, total):
                for j in range(RING * feats // LANES):
                    value = student[big, at, j * LANES:(j + 1) * LANES].astype(jnp.float32)
                    total += value * value
                return total
            total = lax.fori_loop(0, RING, add, jnp.zeros((LANES, LANES), jnp.float32))
            sinv[:, at] = lax.rsqrt(to_lanes(total, jnp.sum) + 1e-06)

    def first_rows(at, carry):
        tinv = lax.rsqrt(jnp.sum(squares[at, :], axis=1, keepdims=True) + 1e-06)
        tseg = left[at, :]
        tops = jnp.full((ROW_BLOCK, LANES), SAFE, jnp.float32)
        count = jnp.zeros((ROW_BLOCK, LANES), jnp.float32)
        for strip in strips:
            support = tseg == sseg[:, strip]
            value = (scaled[at, strip] * tinv * sinv[:, strip] - 1.0) * INV_EPSILON
            value = jnp.where(support, value, FLOOR)
            scaled[at, strip] = value
            tops = jnp.maximum(tops, value)
            count += jnp.where(support, 1.0, 0.0)
        top = jnp.max(tops, axis=1, keepdims=True)
        total = jnp.zeros((ROW_BLOCK, LANES), jnp.float32)
        for strip in strips:
            total += jnp.exp(scaled[at, strip] - top)
        highest[at, :] = jnp.broadcast_to(top, (ROW_BLOCK, LANES))
        right[at, :] = total
        spare[at, :] = count
        return carry

    def rows_of(c):
        return pl.ds(pl.multiple_of(c * chunk, chunk), chunk)

    def product(c, big):
        return lax.dot_general(
            gathered[c, big], student[big], CONTRACT_LAST, preferred_element_type=jnp.float32
        )

    def squared(c, big, total):
        for j in range(RING * feats // LANES):
            value = gathered[c, big, :, j * LANES:(j + 1) * LANES].astype(jnp.float32)
            total += value * value
        return total

    @pl.loop(0, CHUNKS + 4)
    def _(slot):
        def due(stage):
            return (slot >= stage) & (slot < CHUNKS + stage)

        @pl.when(due(0))
        def _():
            theirs[slot] = project(slot, 1 - hid)

        @pl.when(slot == 0)
        def _():
            left[...] = to_rows(tseg_ref[...].reshape(1, rows).astype(jnp.float32))
            pl.semaphore_wait(barrier, 2 * (peers - 1))

        @pl.when(due(0))
        def _():
            core_copy(slot).start()

        @pl.when(due(1))
        def _():
            c = slot - 1
            core_copy(c).wait_recv()
            block(c, major, minor)[...] = (mine[lax.rem(c, 2)] + incoming[c]).astype(jnp.bfloat16)
            own_stage(c)

        @pl.when(due(0))
        def _():
            mine[lax.rem(slot, 2)] = project(slot, hid)

        @pl.when(due(3))
        def _():
            near_stage(slot - 3)

        @pl.when(due(4))
        def _():
            far_stage(slot - 4)

    student_norms()

    @pl.loop(0, CHUNKS)
    def _(c):
        relay_stage(c)
        at = rows_of(c)
        before, after = around(major, -1), around(major, 1)
        scaled[at, :] = product(c, major) + product(c, before) + product(c, after)
        total = squared(c, major, jnp.zeros((chunk, LANES), jnp.float32))
        squares[at, :] = squared(c, after, squared(c, before, total))

    def near_copy(slots, peer, phase, step):
        return pltpu.make_async_remote_copy(
            src_ref=slots.at[REACH], dst_ref=slots.at[REACH - step],
            send_sem=near_send.at[phase], recv_sem=near_recv.at[phase], device_id=peer(step),
        )

    def near_start(slots, peer, phase):
        for step in (-2, -1, 1, 2):
            near_copy(slots, peer, phase, step).start()

    def near_all(slots, peer, phase):
        whole = slots.at[pl.ds(0, 2 * REACH)]
        return pltpu.make_async_remote_copy(
            src_ref=whole, dst_ref=whole,
            send_sem=near_send.at[phase], recv_sem=near_recv.at[phase], device_id=peer(1),
        )

    def spread_copy(ref, peer, phase, step, sends=far_send, recvs=far_recv):
        return pltpu.make_async_remote_copy(
            src_ref=ref, dst_ref=ref, send_sem=sends.at[phase], recv_sem=recvs.at[phase], device_id=peer(step)
        )

    def row_phase(step):
        return CHUNKS + step - 1

    def col_phase(step):
        return CHUNKS + ITERS - 1 + step

    def fold(values):
        return jnp.sum(values.reshape(-1, 8, LANES), axis=0)

    def block_of(c, init, body):
        return by_block(body, init, c * (chunk // ROW_BLOCK), chunk // ROW_BLOCK)

    blank = jnp.zeros((8, LANES), jnp.float32)
    lowest = jnp.full((8, LANES), SAFE, jnp.float32)

    def complete(c):
        last_stage(c)
        at = rows_of(c)
        opposite = around(major, 2)
        scaled[at, :] += product(c, opposite)
        squares[at, :] = squared(c, opposite, squares[at, :])
        block_of(c, None, first_rows)
        row_first[c, REACH] = jnp.concatenate(
            [
                to_lanes(highest[at, :], jnp.max),
                to_lanes(right[at, :], jnp.sum),
                to_lanes(spare[at, :], jnp.sum),
            ],
            axis=1,
        )
        near_start(row_first.at[c], stu_peer, c)

    def held_rows(c):
        return row_first[c, REACH, :, 2 * chunk:] > 0.0

    def first_columns(c):
        near_all(row_first.at[c], stu_peer, c).wait_recv()
        pot, count = merge(row_first[c], chunk)
        pot = jnp.where(held_rows(c), pot, 0.0)
        row_pots[c] = jnp.concatenate([pot, count], axis=1)
        left[rows_of(c), :] = to_rows(pot)

        def largest(at, tops):
            pot = left[at, :]
            new = []
            for strip, top in zip(strips, tops):
                value = scaled[at, strip] + pot
                scaled[at, strip] = value
                new.append(jnp.maximum(top, jnp.max(value.reshape(-1, 8, LANES), axis=0)))
            return new

        tops = [jnp.max(top, axis=0, keepdims=True) for top in block_of(c, [lowest] * len(strips), largest)]

        def terms(at, carry):
            new = []
            for strip, top, (total, count) in zip(strips, tops, carry):
                value = scaled[at, strip]
                term = jnp.exp(value - top)
                scaled[at, strip] = term
                new.append((total + fold(term), count + fold(jnp.where(value > SAFE, 1.0, 0.0))))
            return new

        sums = block_of(c, [(blank, blank)] * len(strips), terms)
        flat = [jnp.sum(value, axis=0, keepdims=True) for k in range(2) for value in [pair[k] for pair in sums]]
        gains[c] = jnp.concatenate(tops + flat, axis=1)

    @pl.loop(0, CHUNKS + 1)
    def _(slot):
        @pl.when(slot < CHUNKS)
        def _():
            complete(slot)

        @pl.when(slot > 0)
        def _():
            first_columns(slot - 1)

    parts = gains[...]
    local_top = jnp.max(parts[:, :, :cols], axis=0)
    local_sum = jnp.sum(parts[:, :, cols:2 * cols] * jnp.exp(parts[:, :, :cols] - local_top), axis=0)
    own_count = jnp.sum(parts[:, :, 2 * cols:], axis=0)
    col_held = own_count > 0.0
    col_first[REACH] = jnp.concatenate([local_top, local_sum, own_count], axis=1)
    near_start(col_first, tea_peer, col_phase(0))

    @pl.loop(0, CHUNKS)
    def _(c):
        near_all(row_first.at[c], stu_peer, c).wait_send()
        core_copy(c).wait_send()
        sent(c)

    near_all(col_first, tea_peer, col_phase(0)).wait_recv()
    col_pot, col_count = merge(col_first[...], cols)
    col_pot = jnp.where(col_held, col_pot, 0.0)
    for c in range(CHUNKS):
        gains[c, :, :cols] = jnp.exp(gains[c, :, :cols] + col_pot)

    def by_chunk_block(body, init=None):
        def step(b, carry):
            at = pl.ds(pl.multiple_of(b * ROW_BLOCK, ROW_BLOCK), ROW_BLOCK)
            return body(at, gains.at[b // (chunk // ROW_BLOCK)], carry)
        return lax.fori_loop(0, blocks, step, init)

    def across(pick):
        return jnp.concatenate([pick(c) for c in range(CHUNKS)], axis=1)

    row_held = across(held_rows)
    first_pot = across(lambda c: row_pots[c, :, :chunk])
    row_count = across(lambda c: row_pots[c, :, chunk:])

    for step in range(1, ITERS):
        last = step == ITERS - 1
        row_slots, col_slots = row_next.at[step - 1], col_next.at[step - 1]

        def later_rows(at, gain, carry):
            total = scaled[at, strips[0]] * gain[:, strips[0]]
            for strip in strips[1:]:
                total += scaled[at, strip] * gain[:, strip]
            right[at, :] = total
            return carry

        by_chunk_block(later_rows)
        row_slots[REACH] = to_lanes(right[...], jnp.sum)
        near_start(row_slots, stu_peer, row_phase(step))
        near_all(row_slots, stu_peer, row_phase(step)).wait_recv()
        factor = row_count / jnp.sum(row_slots[...], axis=0)
        left[...] = to_rows(jnp.where(row_held, factor, 0.0))

        def later_cols(at, gain, sums):
            factor = left[at, :]
            return [
                value + fold(scaled[at, strip] * factor) * gain[:, strip] for strip, value in zip(strips, sums)
            ]

        sums = by_chunk_block(later_cols, [blank] * len(strips))
        total = jnp.concatenate([jnp.sum(value, axis=0, keepdims=True) for value in sums], axis=1)
        if last:
            base = jnp.where(col_held, -col_pot - jnp.log(col_count), SAFE)
            col_last[place] = jnp.concatenate([base, total], axis=1)
            for k in (-2, -1, 1, 2):
                spread_copy(col_last.at[place], tea_peer, col_phase(step), k, near_send, near_recv).start()

            @pl.loop(REACH + 1, peers - REACH)
            def _(k):
                spread_copy(col_last.at[place], tea_peer, 1, k).start()

            row_last[stu] = jnp.where(row_held, first_pot + jnp.log(factor), FLOOR)

            @pl.loop(1, peers)
            def _(k):
                spread_copy(row_last.at[stu], stu_peer, 0, k).start()

            near_cols = spread_copy(
                col_last.at[pl.ds(0, 2 * REACH)], tea_peer, col_phase(step), 1, near_send, near_recv
            )
            near_cols.wait_recv()
            for k in (-2, -1, 1, 2):
                total += col_last[lax.rem(place + k + peers, peers), :, cols:]
        else:
            col_slots[REACH] = total
            near_start(col_slots, tea_peer, col_phase(step))
            near_all(col_slots, tea_peer, col_phase(step)).wait_recv()
            total = jnp.sum(col_slots[...], axis=0)
        fresh = jnp.where(col_held, col_count / total, 1.0)
        col_pot = col_pot + jnp.log(fresh)
        for c in range(CHUNKS):
            gains[c, :, :cols] = gains[c, :, :cols] * fresh

    def finish(at, gain, carry):
        factor = left[at, :]
        for strip in strips:
            plan_ref[at, strip] = (scaled[at, strip] * factor * gain[:, strip]).astype(jnp.bfloat16)
        return carry

    by_chunk_block(finish)
    far_rows = spread_copy(row_last.at[pl.ds(0, peers - 1)], stu_peer, 0, 1)
    far_cols = spread_copy(col_last.at[pl.ds(0, peers - 1 - 2 * REACH)], tea_peer, 1, 1)
    near_cols.wait_send()
    near_all(col_first, tea_peer, col_phase(0)).wait_send()
    for step in range(1, ITERS):
        near_all(row_next.at[step - 1], stu_peer, row_phase(step)).wait_send()
    for step in range(1, ITERS - 1):
        near_all(col_next.at[step - 1], tea_peer, col_phase(step)).wait_send()
    far_rows.wait_recv()
    row_out[...] = jnp.max(row_last[...], axis=0).reshape(rows)
    far_cols.wait_recv()
    base, total = col_last[:, :, :cols], col_last[:, :, cols:]
    top = jnp.max(base, axis=0)
    col_out[...] = -(top + jnp.log(jnp.sum(total * jnp.exp(base - top), axis=0))).reshape(cols)

    far_rows.wait_send()
    far_cols.wait_send()

def hand_over_kernel(plan_ref, row_ref, col_ref, plan_out, row_out, col_out, sems):
    copies = [
        pltpu.make_async_copy(source, target, sems.at[k])
        for k, (source, target) in enumerate(((plan_ref, plan_out), (row_ref, row_out), (col_ref, col_out)))
    ]
    for copy in copies:
        copy.start()
    for copy in copies:
        copy.wait()


def hand_over(*held):
    anywhere = pl.BlockSpec(memory_space=pl.ANY)
    return pl.pallas_call(
        hand_over_kernel,
        out_shape=tuple(jax.ShapeDtypeStruct(value.shape, value.dtype) for value in held),
        in_specs=[pl.BlockSpec(memory_space=pltpu.VMEM)] * len(held),
        out_specs=(anywhere,) * len(held),
        scratch_shapes=[pltpu.SemaphoreType.DMA((len(held),))],
    )(*(pltpu.with_memory_space_constraint(value, pltpu.VMEM) for value in held))


def per_device(peers, teacher_hidden, projection, student_hidden, teacher_segment, student_segment):
    rows, cols, feats = teacher_segment.shape[0], student_segment.shape[0], projection.shape[0]
    depth = teacher_hidden.shape[1]
    chunk = rows // CHUNKS
    vmem = pl.BlockSpec(memory_space=pltpu.VMEM)
    anywhere = pl.BlockSpec(memory_space=pl.ANY)
    plan, row_pot, col_pot = pl.pallas_call(
        functools.partial(kernel, peers),
        out_shape=(
            pltpu.VMEM((rows, cols), jnp.bfloat16),
            pltpu.VMEM((rows,), jnp.float32),
            pltpu.VMEM((cols,), jnp.float32),
        ),
        in_specs=[anywhere] * 3 + [vmem] * 2,
        out_specs=(vmem, vmem, vmem),
        scratch_shapes=[
            pltpu.VMEM((2 * CHUNKS, chunk, depth), jnp.bfloat16),
            pltpu.VMEM((feats, depth), jnp.bfloat16),
            pltpu.VMEM((RING, cols, RING * feats), jnp.bfloat16),
            pltpu.VMEM((CHUNKS, chunk, feats), jnp.float32),
            pltpu.VMEM((2, chunk, feats), jnp.float32),
            pltpu.VMEM((CHUNKS, chunk, feats), jnp.float32),
            pltpu.VMEM((CHUNKS, RING, chunk, RING * feats), jnp.bfloat16),
            pltpu.VMEM((rows, LANES), jnp.float32),
            pltpu.VMEM((rows, LANES), jnp.float32),
            pltpu.VMEM((1, cols), jnp.float32),
            pltpu.VMEM((rows, cols), jnp.float32),
            pltpu.VMEM((rows, LANES), jnp.float32),
            pltpu.VMEM((rows, LANES), jnp.float32),
            pltpu.VMEM((rows, LANES), jnp.float32),
            pltpu.VMEM((CHUNKS, 1, 3 * cols), jnp.float32),
            pltpu.VMEM((CHUNKS, 1, 2 * chunk), jnp.float32),
            pltpu.VMEM((CHUNKS, 2 * REACH + 1, 1, 3 * chunk), jnp.float32),
            pltpu.VMEM((ITERS - 1, 2 * REACH + 1, 1, rows), jnp.float32),
            pltpu.VMEM((peers, 1, rows), jnp.float32),
            pltpu.VMEM((2 * REACH + 1, 1, 3 * cols), jnp.float32),
            pltpu.VMEM((ITERS - 1, 2 * REACH + 1, 1, cols), jnp.float32),
            pltpu.VMEM((peers, 1, 2 * cols), jnp.float32),
            pltpu.SemaphoreType.DMA((2 * CHUNKS,)),
            pltpu.SemaphoreType.DMA((2,)),
            pltpu.SemaphoreType.DMA((CHUNKS,)),
            pltpu.SemaphoreType.DMA((CHUNKS,)),
            pltpu.SemaphoreType.DMA((CHUNKS, 14)),
            pltpu.SemaphoreType.DMA((CHUNKS, 14)),
            pltpu.SemaphoreType.DMA((CHUNKS + 2 * ITERS - 1,)),
            pltpu.SemaphoreType.DMA((CHUNKS + 2 * ITERS - 1,)),
            pltpu.SemaphoreType.DMA((2,)),
            pltpu.SemaphoreType.DMA((2,)),
        ],
        compiler_params=pltpu.CompilerParams(
            collective_id=1, has_side_effects=True, vmem_limit_bytes=60 * 1024 * 1024
        ),
    )(teacher_hidden, projection, student_hidden, teacher_segment, student_segment)
    return hand_over(plan, row_pot, col_pot)


def solution(mesh):
    placed = (P("tea", "hid"), P("stu", "hid"), P("stu", None), P(("tea", "hid")), P("stu"))
    return jax.shard_map(
        functools.partial(per_device, mesh.shape["stu"]),
        mesh=mesh,
        in_specs=placed,
        out_specs=(P(("tea", "hid"), "stu"), P(("tea", "hid")), P("stu")),
        check_vma=False,
    )
```

```python
import functools

import jax
import jax.numpy as jnp
import numpy as np
from jax import lax
from jax.experimental import pallas as pl
from jax.experimental.pallas import tpu as pltpu
from jax.sharding import PartitionSpec as P

ITERS = 3
INV_EPSILON = float(np.float32(1.0) / np.float32(0.004))
FLOOR = -1e30
SAFE = -1e29
LANES = 128
ROW_BLOCK = 128
CHUNKS = 4
RING = 4
TEA_HALF = 4
REACH = 2
CONTRACT_LAST = (((1,), (1,)), ((), ()))


def to_lanes(part, combine):
    return combine(jnp.transpose(part), axis=0, keepdims=True)


def to_rows(vector):
    count = vector.shape[1]
    return jnp.transpose(jnp.broadcast_to(vector, (LANES, count)))


def merge(slots, width):
    tops, sums, counts = (slots[:, :, k * width:(k + 1) * width] for k in range(3))
    top = jnp.max(tops, axis=0)
    total = jnp.sum(sums * jnp.exp(tops - top), axis=0)
    count = jnp.sum(counts, axis=0)
    return jnp.log(count) - (top + jnp.log(total)), count


def kernel(
    peers,
    teacher_ref, proj_ref, student_ref, tseg_ref, sseg_ref,
    plan_ref, row_out, col_out,
    teacher, proj, student, theirs, mine, incoming, gathered, squares, highest, sinv,
    scaled, left, right, spare, gains, row_pots, row_first, row_next, row_last, col_first, col_next, col_last,
    teacher_sem, weight_sem, core_send, core_recv, ring_send, ring_recv, near_send, near_recv, far_send, far_recv, token,
):
    rows, cols = scaled.shape
    feats = proj.shape[0]
    chunk = rows // CHUNKS
    half = chunk // 2
    blocks = rows // ROW_BLOCK
    strips = [slice(k * LANES, (k + 1) * LANES) for k in range(cols // LANES)]
    cores = 2
    stu = lax.axis_index("stu")
    hid = lax.axis_index("hid")
    place = lax.axis_index("tea") * cores + hid

    y, x = stu // RING, lax.rem(stu, RING)
    major, minor = y + hid * (x - y), x + hid * (y - x)

    def stu_of(big, small):
        return (big + hid * (small - big)) * RING + small + hid * (big - small)

    def around(index, step):
        return lax.rem(index + step + RING, RING)

    def stu_peer(step):
        return {"stu": lax.rem(stu + step + peers, peers)}

    def tea_peer(step):
        other = lax.rem(place + step + peers, peers)
        return {"tea": other // cores, "hid": lax.rem(other, cores)}

    def beside(side):
        other = lax.rem(place + 2 * side + peers, peers) // cores
        return {"tea": other, "hid": 1 - hid}

    def pass_token(k):
        for side in (1, -1):
            pl.semaphore_signal(token.at[k], inc=1, device_id=tea_peer(2 * side))

    def teacher_copy(c, whose):
        start = pl.multiple_of((whose * CHUNKS + c) * chunk, chunk)
        return pltpu.make_async_copy(
            teacher_ref.at[pl.ds(start, chunk)], teacher.at[whose * CHUNKS + c], teacher_sem.at[whose * CHUNKS + c]
        )

    proj_copy = pltpu.make_async_copy(proj_ref, proj, weight_sem.at[0])
    proj_copy.start()

    @pl.loop(0, CHUNKS)
    def _(c):
        teacher_copy(c, 1 - hid).start()
        teacher_copy(c, hid).start()

    @pl.loop(0, peers)
    def _(slot):
        big, small = slot // RING, lax.rem(slot, RING)
        source = pl.multiple_of(stu_of(big, small) * feats, feats)
        target = pl.multiple_of(small * feats, feats)
        pltpu.make_async_copy(
            student_ref.at[:, pl.ds(source, feats)], student.at[big, :, pl.ds(target, feats)], weight_sem.at[1]
        ).start()

    sseg = sseg_ref[...].reshape(1, cols).astype(jnp.float32)
    barrier = pltpu.get_barrier_semaphore()

    for side in (1, -1):
        pl.semaphore_signal(barrier, inc=1, device_id={"stu": stu_of(major, around(minor, side))})
        pl.semaphore_signal(barrier, inc=1, device_id={"stu": stu_of(around(major, side), minor)})
        pl.semaphore_signal(barrier, inc=1, device_id=tea_peer(2 * side))
        pl.semaphore_signal(barrier, inc=1, device_id=beside(side))
    pl.semaphore_signal(barrier, inc=1, device_id={"hid": 1 - hid})

    proj_copy.wait()

    def project(c, whose):
        teacher_copy(c, whose).wait()
        return lax.dot_general(
            teacher[whose * CHUNKS + c], proj[...], CONTRACT_LAST, preferred_element_type=jnp.float32
        )

    def core_copy(c):
        return pltpu.make_async_remote_copy(
            src_ref=theirs.at[c], dst_ref=incoming.at[c],
            send_sem=core_send.at[c], recv_sem=core_recv.at[c], device_id={"hid": 1 - hid},
        )

    def ring_copy(c, stage, ref, big, small):
        return pltpu.make_async_remote_copy(
            src_ref=ref, dst_ref=ref,
            send_sem=ring_send.at[c, stage], recv_sem=ring_recv.at[c, stage],
            device_id={"stu": stu_of(around(big, 0), around(small, 0))},
        )

    def block(c, big, small, part=slice(None)):
        return gathered.at[c, around(big, 0), part, pl.ds(pl.multiple_of(around(small, 0) * feats, feats), feats)]

    def bundle(c, big, part=slice(None)):
        return gathered.at[c, around(big, 0), part]

    low, high = pl.ds(0, half), pl.ds(half, half)
    offsets = (0, -1, 1, 2)

    def along_minor(c, k, side, small, part=slice(None)):
        return ring_copy(c, k, block(c, major, small, part), major, minor + side)

    def along_major(c, which, side, big):
        return ring_copy(
            c, 4 + 2 * which + (side < 0), block(c, big, minor + offsets[which]), major + side, minor
        )

    def relay(c, side, big):
        return ring_copy(c, 12 + (side < 0), bundle(c, big, low if side > 0 else high), major + side, minor)

    def send_major(c, which):
        along_major(c, which, 1, major).start()
        along_major(c, which, -1, major).start()

    def own_stage(c):
        along_minor(c, 0, 1, minor).start()
        along_minor(c, 1, -1, minor).start()
        send_major(c, 0)

    def near_stage(c):
        along_minor(c, 0, 1, minor - 1).wait_recv()
        along_minor(c, 2, 1, minor - 1, low).start()
        send_major(c, 1)
        along_minor(c, 1, -1, minor + 1).wait_recv()
        along_minor(c, 3, -1, minor + 1, high).start()
        send_major(c, 2)

    def far_stage(c):
        along_minor(c, 2, 1, minor + 2, low).wait_recv()
        along_minor(c, 3, -1, minor + 2, high).wait_recv()
        send_major(c, 3)

    def relay_stage(c):
        for side in (1, -1):
            for which in range(4):
                along_major(c, which, side, major - side).wait_recv()
            relay(c, side, major - side).start()

    def last_stage(c):
        relay(c, 1, major + 2).wait_recv()
        relay(c, -1, major + 2).wait_recv()

    def sent(c):
        along_minor(c, 0, 1, minor).wait_send()
        along_minor(c, 1, -1, minor).wait_send()
        along_minor(c, 2, 1, minor - 1, low).wait_send()
        along_minor(c, 3, -1, minor + 1, high).wait_send()
        for side in (1, -1):
            for which in range(4):
                along_major(c, which, side, major).wait_send()
            relay(c, side, major - side).wait_send()

    def by_block(body, init=None, first=0, count=blocks):
        def step(b, carry):
            return body(pl.ds(pl.multiple_of(b * ROW_BLOCK, ROW_BLOCK), ROW_BLOCK), carry)
        return lax.fori_loop(first, first + count, step, init)

    def student_norms():
        pltpu.make_async_copy(student, student, weight_sem.at[1]).wait()

        @pl.loop(0, cols // LANES)
        def _(k):
            at = pl.ds(pl.multiple_of(k * LANES, LANES), LANES)
            def add(big, total):
                for j in range(RING * feats // LANES):
                    value = student[big, at, j * LANES:(j + 1) * LANES].astype(jnp.float32)
                    total += value * value
                return total
            total = lax.fori_loop(0, RING, add, jnp.zeros((LANES, LANES), jnp.float32))
            sinv[:, at] = lax.rsqrt(to_lanes(total, jnp.sum) + 1e-06)

    def first_rows(at, carry):
        tinv = lax.rsqrt(jnp.sum(squares[at, :], axis=1, keepdims=True) + 1e-06)
        tseg = left[at, :]
        tops = jnp.full((ROW_BLOCK, LANES), SAFE, jnp.float32)
        count = jnp.zeros((ROW_BLOCK, LANES), jnp.float32)
        for strip in strips:
            support = tseg == sseg[:, strip]
            value = (scaled[at, strip] * tinv * sinv[:, strip] - 1.0) * INV_EPSILON
            value = jnp.where(support, value, FLOOR)
            scaled[at, strip] = value
            tops = jnp.maximum(tops, value)
            count += jnp.where(support, 1.0, 0.0)
        top = jnp.max(tops, axis=1, keepdims=True)
        total = jnp.zeros((ROW_BLOCK, LANES), jnp.float32)
        for strip in strips:
            total += jnp.exp(scaled[at, strip] - top)
        highest[at, :] = jnp.broadcast_to(top, (ROW_BLOCK, LANES))
        right[at, :] = total
        spare[at, :] = count
        return carry

    def rows_of(c):
        return pl.ds(pl.multiple_of(c * chunk, chunk), chunk)

    def product(c, big):
        return lax.dot_general(
            gathered[c, big], student[big], CONTRACT_LAST, preferred_element_type=jnp.float32
        )

    def squared(c, big, total):
        for j in range(RING * feats // LANES):
            value = gathered[c, big, :, j * LANES:(j + 1) * LANES].astype(jnp.float32)
            total += value * value
        return total

    @pl.loop(0, CHUNKS + 4)
    def _(slot):
        def due(stage):
            return (slot >= stage) & (slot < CHUNKS + stage)

        @pl.when(due(0))
        def _():
            theirs[slot] = project(slot, 1 - hid)

        @pl.when(slot == 0)
        def _():
            left[...] = to_rows(tseg_ref[...].reshape(1, rows).astype(jnp.float32))
            pl.semaphore_wait(barrier, 9)
            pass_token(0)

        @pl.when(due(0))
        def _():
            core_copy(slot).start()

        @pl.when(due(1))
        def _():
            c = slot - 1
            core_copy(c).wait_recv()
            block(c, major, minor)[...] = (mine[lax.rem(c, 2)] + incoming[c]).astype(jnp.bfloat16)
            own_stage(c)

        @pl.when(due(0))
        def _():
            mine[lax.rem(slot, 2)] = project(slot, hid)

        @pl.when(due(3))
        def _():
            near_stage(slot - 3)

        @pl.when(due(4))
        def _():
            far_stage(slot - 4)

    student_norms()
    for k in range(1, TEA_HALF):
        pl.semaphore_wait(token.at[k - 1], 2)
        if k < TEA_HALF - 1:
            pass_token(k)

    @pl.loop(0, CHUNKS)
    def _(c):
        relay_stage(c)
        at = rows_of(c)
        before, after = around(major, -1), around(major, 1)
        scaled[at, :] = product(c, major) + product(c, before) + product(c, after)
        total = squared(c, major, jnp.zeros((chunk, LANES), jnp.float32))
        squares[at, :] = squared(c, after, squared(c, before, total))

    def near_copy(slots, peer, phase, step):
        return pltpu.make_async_remote_copy(
            src_ref=slots.at[REACH], dst_ref=slots.at[REACH - step],
            send_sem=near_send.at[phase], recv_sem=near_recv.at[phase], device_id=peer(step),
        )

    def near_start(slots, peer, phase):
        for step in (-2, -1, 1, 2):
            near_copy(slots, peer, phase, step).start()

    def near_all(slots, peer, phase):
        whole = slots.at[pl.ds(0, 2 * REACH)]
        return pltpu.make_async_remote_copy(
            src_ref=whole, dst_ref=whole,
            send_sem=near_send.at[phase], recv_sem=near_recv.at[phase], device_id=peer(1),
        )

    def spread_copy(ref, peer, phase, step, sends=far_send, recvs=far_recv):
        return pltpu.make_async_remote_copy(
            src_ref=ref, dst_ref=ref, send_sem=sends.at[phase], recv_sem=recvs.at[phase], device_id=peer(step)
        )

    def row_phase(step):
        return CHUNKS + step - 1

    def col_phase(step):
        return CHUNKS + ITERS - 1 + step

    def fold(values):
        return jnp.sum(values.reshape(-1, 8, LANES), axis=0)

    def block_of(c, init, body):
        return by_block(body, init, c * (chunk // ROW_BLOCK), chunk // ROW_BLOCK)

    blank = jnp.zeros((8, LANES), jnp.float32)
    lowest = jnp.full((8, LANES), SAFE, jnp.float32)

    def complete(c):
        last_stage(c)
        at = rows_of(c)
        opposite = around(major, 2)
        scaled[at, :] += product(c, opposite)
        squares[at, :] = squared(c, opposite, squares[at, :])
        block_of(c, None, first_rows)
        row_first[c, REACH] = jnp.concatenate(
            [
                to_lanes(highest[at, :], jnp.max),
                to_lanes(right[at, :], jnp.sum),
                to_lanes(spare[at, :], jnp.sum),
            ],
            axis=1,
        )
        near_start(row_first.at[c], stu_peer, c)

    def held_rows(c):
        return row_first[c, REACH, :, 2 * chunk:] > 0.0

    def first_columns(c):
        near_all(row_first.at[c], stu_peer, c).wait_recv()
        pot, count = merge(row_first[c], chunk)
        pot = jnp.where(held_rows(c), pot, 0.0)
        row_pots[c] = jnp.concatenate([pot, count], axis=1)
        left[rows_of(c), :] = to_rows(pot)

        def largest(at, tops):
            pot = left[at, :]
            new = []
            for strip, top in zip(strips, tops):
                value = scaled[at, strip] + pot
                scaled[at, strip] = value
                new.append(jnp.maximum(top, jnp.max(value.reshape(-1, 8, LANES), axis=0)))
            return new

        tops = [jnp.max(top, axis=0, keepdims=True) for top in block_of(c, [lowest] * len(strips), largest)]

        def terms(at, carry):
            new = []
            for strip, top, (total, count) in zip(strips, tops, carry):
                value = scaled[at, strip]
                term = jnp.exp(value - top)
                scaled[at, strip] = term
                new.append((total + fold(term), count + fold(jnp.where(value > SAFE, 1.0, 0.0))))
            return new

        sums = block_of(c, [(blank, blank)] * len(strips), terms)
        flat = [jnp.sum(value, axis=0, keepdims=True) for k in range(2) for value in [pair[k] for pair in sums]]
        gains[c] = jnp.concatenate(tops + flat, axis=1)

    @pl.loop(0, CHUNKS + 1)
    def _(slot):
        @pl.when(slot < CHUNKS)
        def _():
            complete(slot)

        @pl.when(slot > 0)
        def _():
            first_columns(slot - 1)

    parts = gains[...]
    local_top = jnp.max(parts[:, :, :cols], axis=0)
    local_sum = jnp.sum(parts[:, :, cols:2 * cols] * jnp.exp(parts[:, :, :cols] - local_top), axis=0)
    own_count = jnp.sum(parts[:, :, 2 * cols:], axis=0)
    col_held = own_count > 0.0
    col_first[REACH] = jnp.concatenate([local_top, local_sum, own_count], axis=1)
    near_start(col_first, tea_peer, col_phase(0))

    @pl.loop(0, CHUNKS)
    def _(c):
        near_all(row_first.at[c], stu_peer, c).wait_send()
        core_copy(c).wait_send()
        sent(c)

    near_all(col_first, tea_peer, col_phase(0)).wait_recv()
    col_pot, col_count = merge(col_first[...], cols)
    col_pot = jnp.where(col_held, col_pot, 0.0)
    for c in range(CHUNKS):
        gains[c, :, :cols] = jnp.exp(gains[c, :, :cols] + col_pot)

    def by_chunk_block(body, init=None):
        def step(b, carry):
            at = pl.ds(pl.multiple_of(b * ROW_BLOCK, ROW_BLOCK), ROW_BLOCK)
            return body(at, gains.at[b // (chunk // ROW_BLOCK)], carry)
        return lax.fori_loop(0, blocks, step, init)

    def across(pick):
        return jnp.concatenate([pick(c) for c in range(CHUNKS)], axis=1)

    row_held = across(held_rows)
    first_pot = across(lambda c: row_pots[c, :, :chunk])
    row_count = across(lambda c: row_pots[c, :, chunk:])

    for step in range(1, ITERS):
        last = step == ITERS - 1
        row_slots, col_slots = row_next.at[step - 1], col_next.at[step - 1]

        def later_rows(at, gain, carry):
            total = scaled[at, strips[0]] * gain[:, strips[0]]
            for strip in strips[1:]:
                total += scaled[at, strip] * gain[:, strip]
            right[at, :] = total
            return carry

        by_chunk_block(later_rows)
        row_slots[REACH] = to_lanes(right[...], jnp.sum)
        near_start(row_slots, stu_peer, row_phase(step))
        near_all(row_slots, stu_peer, row_phase(step)).wait_recv()
        factor = row_count / jnp.sum(row_slots[...], axis=0)
        left[...] = to_rows(jnp.where(row_held, factor, 0.0))

        def later_cols(at, gain, sums):
            factor = left[at, :]
            return [
                value + fold(scaled[at, strip] * factor) * gain[:, strip] for strip, value in zip(strips, sums)
            ]

        sums = by_chunk_block(later_cols, [blank] * len(strips))
        total = jnp.concatenate([jnp.sum(value, axis=0, keepdims=True) for value in sums], axis=1)
        if last:
            base = jnp.where(col_held, -col_pot - jnp.log(col_count), SAFE)
            col_last[place] = jnp.concatenate([base, total], axis=1)
            for k in (-2, -1, 1, 2):
                spread_copy(col_last.at[place], tea_peer, col_phase(step), k, near_send, near_recv).start()

            @pl.loop(REACH + 1, peers - REACH)
            def _(k):
                spread_copy(col_last.at[place], tea_peer, 1, k).start()

            row_last[stu] = jnp.where(row_held, first_pot + jnp.log(factor), FLOOR)

            @pl.loop(1, peers)
            def _(k):
                spread_copy(row_last.at[stu], stu_peer, 0, k).start()

            near_cols = spread_copy(
                col_last.at[pl.ds(0, 2 * REACH)], tea_peer, col_phase(step), 1, near_send, near_recv
            )
            near_cols.wait_recv()
            for k in (-2, -1, 1, 2):
                total += col_last[lax.rem(place + k + peers, peers), :, cols:]
        else:
            col_slots[REACH] = total
            near_start(col_slots, tea_peer, col_phase(step))
            near_all(col_slots, tea_peer, col_phase(step)).wait_recv()
            total = jnp.sum(col_slots[...], axis=0)
        fresh = jnp.where(col_held, col_count / total, 1.0)
        col_pot = col_pot + jnp.log(fresh)
        for c in range(CHUNKS):
            gains[c, :, :cols] = gains[c, :, :cols] * fresh

    def finish(at, gain, carry):
        factor = left[at, :]
        for strip in strips:
            plan_ref[at, strip] = (scaled[at, strip] * factor * gain[:, strip]).astype(jnp.bfloat16)
        return carry

    by_chunk_block(finish)
    far_rows = spread_copy(row_last.at[pl.ds(0, peers - 1)], stu_peer, 0, 1)
    far_cols = spread_copy(col_last.at[pl.ds(0, peers - 1 - 2 * REACH)], tea_peer, 1, 1)
    near_cols.wait_send()
    near_all(col_first, tea_peer, col_phase(0)).wait_send()
    for step in range(1, ITERS):
        near_all(row_next.at[step - 1], stu_peer, row_phase(step)).wait_send()
    for step in range(1, ITERS - 1):
        near_all(col_next.at[step - 1], tea_peer, col_phase(step)).wait_send()
    far_rows.wait_recv()
    row_out[...] = jnp.max(row_last[...], axis=0).reshape(rows)
    far_cols.wait_recv()
    base, total = col_last[:, :, :cols], col_last[:, :, cols:]
    top = jnp.max(base, axis=0)
    col_out[...] = -(top + jnp.log(jnp.sum(total * jnp.exp(base - top), axis=0))).reshape(cols)

    far_rows.wait_send()
    far_cols.wait_send()

def hand_over_kernel(plan_ref, row_ref, col_ref, plan_out, row_out, col_out, sems):
    copies = [
        pltpu.make_async_copy(source, target, sems.at[k])
        for k, (source, target) in enumerate(((plan_ref, plan_out), (row_ref, row_out), (col_ref, col_out)))
    ]
    for copy in copies:
        copy.start()
    for copy in copies:
        copy.wait()


def hand_over(*held):
    anywhere = pl.BlockSpec(memory_space=pl.ANY)
    return pl.pallas_call(
        hand_over_kernel,
        out_shape=tuple(jax.ShapeDtypeStruct(value.shape, value.dtype) for value in held),
        in_specs=[pl.BlockSpec(memory_space=pltpu.VMEM)] * len(held),
        out_specs=(anywhere,) * len(held),
        scratch_shapes=[pltpu.SemaphoreType.DMA((len(held),))],
    )(*(pltpu.with_memory_space_constraint(value, pltpu.VMEM) for value in held))


def per_device(peers, teacher_hidden, projection, student_hidden, teacher_segment, student_segment):
    rows, cols, feats = teacher_segment.shape[0], student_segment.shape[0], projection.shape[0]
    depth = teacher_hidden.shape[1]
    chunk = rows // CHUNKS
    vmem = pl.BlockSpec(memory_space=pltpu.VMEM)
    anywhere = pl.BlockSpec(memory_space=pl.ANY)
    plan, row_pot, col_pot = pl.pallas_call(
        functools.partial(kernel, peers),
        out_shape=(
            pltpu.VMEM((rows, cols), jnp.bfloat16),
            pltpu.VMEM((rows,), jnp.float32),
            pltpu.VMEM((cols,), jnp.float32),
        ),
        in_specs=[anywhere] * 3 + [vmem] * 2,
        out_specs=(vmem, vmem, vmem),
        scratch_shapes=[
            pltpu.VMEM((2 * CHUNKS, chunk, depth), jnp.bfloat16),
            pltpu.VMEM((feats, depth), jnp.bfloat16),
            pltpu.VMEM((RING, cols, RING * feats), jnp.bfloat16),
            pltpu.VMEM((CHUNKS, chunk, feats), jnp.float32),
            pltpu.VMEM((2, chunk, feats), jnp.float32),
            pltpu.VMEM((CHUNKS, chunk, feats), jnp.float32),
            pltpu.VMEM((CHUNKS, RING, chunk, RING * feats), jnp.bfloat16),
            pltpu.VMEM((rows, LANES), jnp.float32),
            pltpu.VMEM((rows, LANES), jnp.float32),
            pltpu.VMEM((1, cols), jnp.float32),
            pltpu.VMEM((rows, cols), jnp.float32),
            pltpu.VMEM((rows, LANES), jnp.float32),
            pltpu.VMEM((rows, LANES), jnp.float32),
            pltpu.VMEM((rows, LANES), jnp.float32),
            pltpu.VMEM((CHUNKS, 1, 3 * cols), jnp.float32),
            pltpu.VMEM((CHUNKS, 1, 2 * chunk), jnp.float32),
            pltpu.VMEM((CHUNKS, 2 * REACH + 1, 1, 3 * chunk), jnp.float32),
            pltpu.VMEM((ITERS - 1, 2 * REACH + 1, 1, rows), jnp.float32),
            pltpu.VMEM((peers, 1, rows), jnp.float32),
            pltpu.VMEM((2 * REACH + 1, 1, 3 * cols), jnp.float32),
            pltpu.VMEM((ITERS - 1, 2 * REACH + 1, 1, cols), jnp.float32),
            pltpu.VMEM((peers, 1, 2 * cols), jnp.float32),
            pltpu.SemaphoreType.DMA((2 * CHUNKS,)),
            pltpu.SemaphoreType.DMA((2,)),
            pltpu.SemaphoreType.DMA((CHUNKS,)),
            pltpu.SemaphoreType.DMA((CHUNKS,)),
            pltpu.SemaphoreType.DMA((CHUNKS, 14)),
            pltpu.SemaphoreType.DMA((CHUNKS, 14)),
            pltpu.SemaphoreType.DMA((CHUNKS + 2 * ITERS - 1,)),
            pltpu.SemaphoreType.DMA((CHUNKS + 2 * ITERS - 1,)),
            pltpu.SemaphoreType.DMA((2,)),
            pltpu.SemaphoreType.DMA((2,)),
            pltpu.SemaphoreType.REGULAR((TEA_HALF - 1,)),
        ],
        compiler_params=pltpu.CompilerParams(
            collective_id=1, has_side_effects=True, vmem_limit_bytes=60 * 1024 * 1024
        ),
    )(teacher_hidden, projection, student_hidden, teacher_segment, student_segment)
    return hand_over(plan, row_pot, col_pot)


def solution(mesh):
    placed = (P("tea", "hid"), P("stu", "hid"), P("stu", None), P(("tea", "hid")), P("stu"))
    return jax.shard_map(
        functools.partial(per_device, mesh.shape["stu"]),
        mesh=mesh,
        in_specs=placed,
        out_specs=(P(("tea", "hid"), "stu"), P(("tea", "hid")), P("stu")),
        check_vma=False,
    )
```

```python
import functools

import jax
import jax.numpy as jnp
import numpy as np
from jax import lax
from jax.experimental import pallas as pl
from jax.experimental.pallas import tpu as pltpu
from jax.sharding import PartitionSpec as P

ITERS = 3
INV_EPSILON = float(np.float32(1.0) / np.float32(0.004))
FLOOR = -1e30
SAFE = -1e29
LANES = 128
ROW_BLOCK = 128
CHUNKS = 4
RING = 4
TEA_HALF = 4
REACH = 2
CONTRACT_LAST = (((1,), (1,)), ((), ()))


def to_lanes(part, combine):
    return combine(jnp.transpose(part), axis=0, keepdims=True)


def to_rows(vector):
    count = vector.shape[1]
    return jnp.transpose(jnp.broadcast_to(vector, (LANES, count)))


def merge(slots, width):
    tops, sums, counts = (slots[:, :, k * width:(k + 1) * width] for k in range(3))
    top = jnp.max(tops, axis=0)
    total = jnp.sum(sums * jnp.exp(tops - top), axis=0)
    count = jnp.sum(counts, axis=0)
    return jnp.log(count) - (top + jnp.log(total)), count


def kernel(
    peers,
    teacher_ref, proj_ref, student_ref, tseg_ref, sseg_ref,
    plan_ref, row_out, col_out,
    teacher, proj, student, theirs, mine, incoming, gathered, squares, highest, sinv,
    scaled, left, right, spare, gains, row_pots, row_first, row_next, row_last, col_first, col_next, col_last,
    teacher_sem, weight_sem, core_send, core_recv, ring_send, ring_recv, near_send, near_recv, far_send, far_recv, token,
):
    rows, cols = scaled.shape
    feats = proj.shape[0]
    chunk = rows // CHUNKS
    half = chunk // 2
    blocks = rows // ROW_BLOCK
    strips = [slice(k * LANES, (k + 1) * LANES) for k in range(cols // LANES)]
    cores = 2
    stu = lax.axis_index("stu")
    hid = lax.axis_index("hid")
    place = lax.axis_index("tea") * cores + hid

    y, x = stu // RING, lax.rem(stu, RING)
    major, minor = y + hid * (x - y), x + hid * (y - x)

    def stu_of(big, small):
        return (big + hid * (small - big)) * RING + small + hid * (big - small)

    def around(index, step):
        return lax.rem(index + step + RING, RING)

    def stu_peer(step):
        return {"stu": lax.rem(stu + step + peers, peers)}

    def tea_peer(step):
        other = lax.rem(place + step + peers, peers)
        return {"tea": other // cores, "hid": lax.rem(other, cores)}

    def beside(side):
        other = lax.rem(place + 2 * side + peers, peers) // cores
        return {"tea": other, "hid": 1 - hid}

    def pass_token(k):
        for side in (1, -1):
            pl.semaphore_signal(token.at[k], inc=1, device_id=tea_peer(2 * side))

    def teacher_copy(c, whose):
        start = pl.multiple_of((whose * CHUNKS + c) * chunk, chunk)
        return pltpu.make_async_copy(
            teacher_ref.at[pl.ds(start, chunk)], teacher.at[whose * CHUNKS + c], teacher_sem.at[whose * CHUNKS + c]
        )

    proj_copy = pltpu.make_async_copy(proj_ref, proj, weight_sem.at[0])
    proj_copy.start()

    @pl.loop(0, CHUNKS)
    def _(c):
        teacher_copy(c, 1 - hid).start()
        teacher_copy(c, hid).start()

    @pl.loop(0, peers)
    def _(slot):
        big, small = slot // RING, lax.rem(slot, RING)
        source = pl.multiple_of(stu_of(big, small) * feats, feats)
        target = pl.multiple_of(small * feats, feats)
        pltpu.make_async_copy(
            student_ref.at[:, pl.ds(source, feats)], student.at[big, :, pl.ds(target, feats)], weight_sem.at[1]
        ).start()

    sseg = sseg_ref[...].reshape(1, cols).astype(jnp.float32)
    barrier = pltpu.get_barrier_semaphore()

    for side in (1, -1):
        pl.semaphore_signal(barrier, inc=1, device_id={"stu": stu_of(major, around(minor, side))})
        pl.semaphore_signal(barrier, inc=1, device_id={"stu": stu_of(around(major, side), minor)})
        pl.semaphore_signal(barrier, inc=1, device_id=tea_peer(2 * side))
        pl.semaphore_signal(barrier, inc=1, device_id=beside(side))
    pl.semaphore_signal(barrier, inc=1, device_id={"hid": 1 - hid})

    proj_copy.wait()

    def project(c, whose):
        teacher_copy(c, whose).wait()
        return lax.dot_general(
            teacher[whose * CHUNKS + c], proj[...], CONTRACT_LAST, preferred_element_type=jnp.float32
        )

    def core_copy(c):
        return pltpu.make_async_remote_copy(
            src_ref=theirs.at[c], dst_ref=incoming.at[c],
            send_sem=core_send.at[c], recv_sem=core_recv.at[c], device_id={"hid": 1 - hid},
        )

    def ring_copy(c, stage, ref, big, small):
        return pltpu.make_async_remote_copy(
            src_ref=ref, dst_ref=ref,
            send_sem=ring_send.at[c, stage], recv_sem=ring_recv.at[c, stage],
            device_id={"stu": stu_of(around(big, 0), around(small, 0))},
        )

    def block(c, big, small, part=slice(None)):
        return gathered.at[c, around(big, 0), part, pl.ds(pl.multiple_of(around(small, 0) * feats, feats), feats)]

    def bundle(c, big, part=slice(None)):
        return gathered.at[c, around(big, 0), part]

    low, high = pl.ds(0, half), pl.ds(half, half)
    offsets = (0, -1, 1, 2)

    def along_minor(c, k, side, small, part=slice(None)):
        return ring_copy(c, k, block(c, major, small, part), major, minor + side)

    def along_major(c, which, side, big):
        return ring_copy(
            c, 4 + 2 * which + (side < 0), block(c, big, minor + offsets[which]), major + side, minor
        )

    def relay(c, side, big):
        return ring_copy(c, 12 + (side < 0), bundle(c, big, low if side > 0 else high), major + side, minor)

    def send_major(c, which):
        along_major(c, which, 1, major).start()
        along_major(c, which, -1, major).start()

    def own_stage(c):
        along_minor(c, 0, 1, minor).start()
        along_minor(c, 1, -1, minor).start()
        send_major(c, 0)

    def near_stage(c):
        along_minor(c, 0, 1, minor - 1).wait_recv()
        along_minor(c, 2, 1, minor - 1, low).start()
        send_major(c, 1)
        along_minor(c, 1, -1, minor + 1).wait_recv()
        along_minor(c, 3, -1, minor + 1, high).start()
        send_major(c, 2)

    def far_stage(c):
        along_minor(c, 2, 1, minor + 2, low).wait_recv()
        along_minor(c, 3, -1, minor + 2, high).wait_recv()
        send_major(c, 3)

    def relay_stage(c):
        for side in (1, -1):
            for which in range(4):
                along_major(c, which, side, major - side).wait_recv()
            relay(c, side, major - side).start()

    def last_stage(c):
        relay(c, 1, major + 2).wait_recv()
        relay(c, -1, major + 2).wait_recv()

    def sent(c):
        along_minor(c, 0, 1, minor).wait_send()
        along_minor(c, 1, -1, minor).wait_send()
        along_minor(c, 2, 1, minor - 1, low).wait_send()
        along_minor(c, 3, -1, minor + 1, high).wait_send()
        for side in (1, -1):
            for which in range(4):
                along_major(c, which, side, major).wait_send()
            relay(c, side, major - side).wait_send()

    def by_block(body, init=None, first=0, count=blocks):
        def step(b, carry):
            return body(pl.ds(pl.multiple_of(b * ROW_BLOCK, ROW_BLOCK), ROW_BLOCK), carry)
        return lax.fori_loop(first, first + count, step, init)

    def student_norms():
        pltpu.make_async_copy(student, student, weight_sem.at[1]).wait()

        @pl.loop(0, cols // LANES)
        def _(k):
            at = pl.ds(pl.multiple_of(k * LANES, LANES), LANES)
            def add(big, total):
                for j in range(RING * feats // LANES):
                    value = student[big, at, j * LANES:(j + 1) * LANES].astype(jnp.float32)
                    total += value * value
                return total
            total = lax.fori_loop(0, RING, add, jnp.zeros((LANES, LANES), jnp.float32))
            sinv[:, at] = lax.rsqrt(to_lanes(total, jnp.sum) + 1e-06)

    def first_rows(at, carry):
        tinv = lax.rsqrt(jnp.sum(squares[at, :], axis=1, keepdims=True) + 1e-06)
        tseg = left[at, :]
        tops = jnp.full((ROW_BLOCK, LANES), SAFE, jnp.float32)
        for strip in strips:
            support = tseg == sseg[:, strip]
            value = (scaled[at, strip] * tinv * sinv[:, strip] - 1.0) * INV_EPSILON
            value = jnp.where(support, value, FLOOR)
            scaled[at, strip] = value
            tops = jnp.maximum(tops, value)
        top = jnp.max(tops, axis=1, keepdims=True)
        total = jnp.zeros((ROW_BLOCK, LANES), jnp.float32)
        for strip in strips:
            total += jnp.exp(scaled[at, strip] - top)
        highest[at, :] = jnp.broadcast_to(top, (ROW_BLOCK, LANES))
        right[at, :] = total
        return carry

    def count_rows(at, carry):
        tseg = left[at, :]
        count = jnp.zeros((ROW_BLOCK, LANES), jnp.float32)
        for strip in strips:
            count += jnp.where(tseg == sseg[:, strip], 1.0, 0.0)
        spare[at, :] = count
        return carry

    def rows_of(c):
        return pl.ds(pl.multiple_of(c * chunk, chunk), chunk)

    def product(c, big):
        return lax.dot_general(
            gathered[c, big], student[big], CONTRACT_LAST, preferred_element_type=jnp.float32
        )

    def squared(c, big, total):
        for j in range(RING * feats // LANES):
            value = gathered[c, big, :, j * LANES:(j + 1) * LANES].astype(jnp.float32)
            total += value * value
        return total

    @pl.loop(0, CHUNKS + 4)
    def _(slot):
        def due(stage):
            return (slot >= stage) & (slot < CHUNKS + stage)

        @pl.when(due(0))
        def _():
            theirs[slot] = project(slot, 1 - hid)

        @pl.when(slot == 0)
        def _():
            left[...] = to_rows(tseg_ref[...].reshape(1, rows).astype(jnp.float32))
            pl.semaphore_wait(barrier, 9)
            pass_token(0)

        @pl.when(due(0))
        def _():
            core_copy(slot).start()

        @pl.when(due(1))
        def _():
            c = slot - 1
            core_copy(c).wait_recv()
            block(c, major, minor)[...] = (mine[lax.rem(c, 2)] + incoming[c]).astype(jnp.bfloat16)
            own_stage(c)

        @pl.when(due(0))
        def _():
            mine[lax.rem(slot, 2)] = project(slot, hid)

        @pl.when(due(3))
        def _():
            near_stage(slot - 3)

        @pl.when(due(4))
        def _():
            far_stage(slot - 4)

    student_norms()
    for k in range(1, TEA_HALF):
        pl.semaphore_wait(token.at[k - 1], 2)
        if k < TEA_HALF - 1:
            pass_token(k)

    @pl.loop(0, CHUNKS)
    def _(c):
        relay_stage(c)
        at = rows_of(c)
        before, after = around(major, -1), around(major, 1)
        scaled[at, :] = product(c, major) + product(c, before) + product(c, after)
        total = squared(c, major, jnp.zeros((chunk, LANES), jnp.float32))
        squares[at, :] = squared(c, after, squared(c, before, total))
        by_block(count_rows, None, c * (chunk // ROW_BLOCK), chunk // ROW_BLOCK)
        row_first[c, REACH, :, 2 * chunk:] = to_lanes(spare[at, :], jnp.sum)

    def near_copy(slots, peer, phase, step):
        return pltpu.make_async_remote_copy(
            src_ref=slots.at[REACH], dst_ref=slots.at[REACH - step],
            send_sem=near_send.at[phase], recv_sem=near_recv.at[phase], device_id=peer(step),
        )

    def near_start(slots, peer, phase):
        for step in (-2, 2, -1, 1):
            near_copy(slots, peer, phase, step).start()

    def near_all(slots, peer, phase):
        whole = slots.at[pl.ds(0, 2 * REACH)]
        return pltpu.make_async_remote_copy(
            src_ref=whole, dst_ref=whole,
            send_sem=near_send.at[phase], recv_sem=near_recv.at[phase], device_id=peer(1),
        )

    def spread_copy(ref, peer, phase, step, sends=far_send, recvs=far_recv):
        return pltpu.make_async_remote_copy(
            src_ref=ref, dst_ref=ref, send_sem=sends.at[phase], recv_sem=recvs.at[phase], device_id=peer(step)
        )

    def row_phase(step):
        return CHUNKS + step - 1

    def col_phase(step):
        return CHUNKS + ITERS - 1 + step

    def fold(values):
        return jnp.sum(values.reshape(-1, 8, LANES), axis=0)

    def block_of(c, init, body):
        return by_block(body, init, c * (chunk // ROW_BLOCK), chunk // ROW_BLOCK)

    blank = jnp.zeros((8, LANES), jnp.float32)
    lowest = jnp.full((8, LANES), SAFE, jnp.float32)

    def complete(c):
        last_stage(c)
        at = rows_of(c)
        opposite = around(major, 2)
        scaled[at, :] += product(c, opposite)
        squares[at, :] = squared(c, opposite, squares[at, :])
        block_of(c, None, first_rows)
        row_first[c, REACH] = jnp.concatenate(
            [
                to_lanes(highest[at, :], jnp.max),
                to_lanes(right[at, :], jnp.sum),
                row_first[c, REACH, :, 2 * chunk:],
            ],
            axis=1,
        )
        near_start(row_first.at[c], stu_peer, c)

    def held_rows(c):
        return row_first[c, REACH, :, 2 * chunk:] > 0.0

    def first_columns(c):
        near_all(row_first.at[c], stu_peer, c).wait_recv()
        pot, count = merge(row_first[c], chunk)
        pot = jnp.where(held_rows(c), pot, 0.0)
        row_pots[c] = jnp.concatenate([pot, count], axis=1)
        left[rows_of(c), :] = to_rows(pot)

        def largest(at, tops):
            pot = left[at, :]
            new = []
            for strip, top in zip(strips, tops):
                value = scaled[at, strip] + pot
                scaled[at, strip] = value
                new.append(jnp.maximum(top, jnp.max(value.reshape(-1, 8, LANES), axis=0)))
            return new

        tops = [jnp.max(top, axis=0, keepdims=True) for top in block_of(c, [lowest] * len(strips), largest)]

        def terms(at, carry):
            new = []
            for strip, top, (total, count) in zip(strips, tops, carry):
                value = scaled[at, strip]
                term = jnp.exp(value - top)
                scaled[at, strip] = term
                new.append((total + fold(term), count + fold(jnp.where(value > SAFE, 1.0, 0.0))))
            return new

        sums = block_of(c, [(blank, blank)] * len(strips), terms)
        flat = [jnp.sum(value, axis=0, keepdims=True) for k in range(2) for value in [pair[k] for pair in sums]]
        gains[c] = jnp.concatenate(tops + flat, axis=1)

    @pl.loop(0, CHUNKS + 1)
    def _(slot):
        @pl.when(slot < CHUNKS)
        def _():
            complete(slot)

        @pl.when(slot > 0)
        def _():
            first_columns(slot - 1)

    parts = gains[...]
    local_top = jnp.max(parts[:, :, :cols], axis=0)
    local_sum = jnp.sum(parts[:, :, cols:2 * cols] * jnp.exp(parts[:, :, :cols] - local_top), axis=0)
    own_count = jnp.sum(parts[:, :, 2 * cols:], axis=0)
    col_held = own_count > 0.0
    col_first[REACH] = jnp.concatenate([local_top, local_sum, own_count], axis=1)
    near_start(col_first, tea_peer, col_phase(0))

    @pl.loop(0, CHUNKS)
    def _(c):
        near_all(row_first.at[c], stu_peer, c).wait_send()
        core_copy(c).wait_send()
        sent(c)

    near_all(col_first, tea_peer, col_phase(0)).wait_recv()
    col_pot, col_count = merge(col_first[...], cols)
    col_pot = jnp.where(col_held, col_pot, 0.0)
    for c in range(CHUNKS):
        gains[c, :, :cols] = jnp.exp(gains[c, :, :cols] + col_pot)

    def by_chunk_block(body, init=None):
        def step(b, carry):
            at = pl.ds(pl.multiple_of(b * ROW_BLOCK, ROW_BLOCK), ROW_BLOCK)
            return body(at, gains.at[b // (chunk // ROW_BLOCK)], carry)
        return lax.fori_loop(0, blocks, step, init)

    def across(pick):
        return jnp.concatenate([pick(c) for c in range(CHUNKS)], axis=1)

    row_held = across(held_rows)
    first_pot = across(lambda c: row_pots[c, :, :chunk])
    row_count = across(lambda c: row_pots[c, :, chunk:])

    for step in range(1, ITERS):
        last = step == ITERS - 1
        row_slots, col_slots = row_next.at[step - 1], col_next.at[step - 1]

        def later_rows(at, gain, carry):
            total = scaled[at, strips[0]] * gain[:, strips[0]]
            for strip in strips[1:]:
                total += scaled[at, strip] * gain[:, strip]
            right[at, :] = total
            return carry

        by_chunk_block(later_rows)
        row_slots[REACH] = to_lanes(right[...], jnp.sum)
        near_start(row_slots, stu_peer, row_phase(step))
        near_all(row_slots, stu_peer, row_phase(step)).wait_recv()
        factor = row_count / jnp.sum(row_slots[...], axis=0)
        left[...] = to_rows(jnp.where(row_held, factor, 0.0))

        def later_cols(at, gain, sums):
            factor = left[at, :]
            return [
                value + fold(scaled[at, strip] * factor) * gain[:, strip] for strip, value in zip(strips, sums)
            ]

        sums = by_chunk_block(later_cols, [blank] * len(strips))
        total = jnp.concatenate([jnp.sum(value, axis=0, keepdims=True) for value in sums], axis=1)
        if last:
            base = jnp.where(col_held, -col_pot - jnp.log(col_count), SAFE)
            col_last[place] = jnp.concatenate([base, total], axis=1)
            for k in (-2, 2, -1, 1):
                spread_copy(col_last.at[place], tea_peer, col_phase(step), k, near_send, near_recv).start()

            @pl.loop(REACH + 1, peers - REACH)
            def _(k):
                spread_copy(col_last.at[place], tea_peer, 1, k).start()

            row_last[stu] = jnp.where(row_held, first_pot + jnp.log(factor), FLOOR)

            @pl.loop(1, peers)
            def _(k):
                spread_copy(row_last.at[stu], stu_peer, 0, k).start()

            near_cols = spread_copy(
                col_last.at[pl.ds(0, 2 * REACH)], tea_peer, col_phase(step), 1, near_send, near_recv
            )
            near_cols.wait_recv()
            for k in (-2, -1, 1, 2):
                total += col_last[lax.rem(place + k + peers, peers), :, cols:]
        else:
            col_slots[REACH] = total
            near_start(col_slots, tea_peer, col_phase(step))
            near_all(col_slots, tea_peer, col_phase(step)).wait_recv()
            total = jnp.sum(col_slots[...], axis=0)
        fresh = jnp.where(col_held, col_count / total, 1.0)
        col_pot = col_pot + jnp.log(fresh)
        for c in range(CHUNKS):
            gains[c, :, :cols] = gains[c, :, :cols] * fresh

    def finish(at, gain, carry):
        factor = left[at, :]
        for strip in strips:
            plan_ref[at, strip] = (scaled[at, strip] * factor * gain[:, strip]).astype(jnp.bfloat16)
        return carry

    by_chunk_block(finish)
    far_rows = spread_copy(row_last.at[pl.ds(0, peers - 1)], stu_peer, 0, 1)
    far_cols = spread_copy(col_last.at[pl.ds(0, peers - 1 - 2 * REACH)], tea_peer, 1, 1)
    near_cols.wait_send()
    near_all(col_first, tea_peer, col_phase(0)).wait_send()
    for step in range(1, ITERS):
        near_all(row_next.at[step - 1], stu_peer, row_phase(step)).wait_send()
    for step in range(1, ITERS - 1):
        near_all(col_next.at[step - 1], tea_peer, col_phase(step)).wait_send()
    far_rows.wait_recv()
    row_out[...] = jnp.max(row_last[...], axis=0).reshape(rows)
    far_cols.wait_recv()
    base, total = col_last[:, :, :cols], col_last[:, :, cols:]
    top = jnp.max(base, axis=0)
    col_out[...] = -(top + jnp.log(jnp.sum(total * jnp.exp(base - top), axis=0))).reshape(cols)

    far_rows.wait_send()
    far_cols.wait_send()

def hand_over_kernel(plan_ref, row_ref, col_ref, plan_out, row_out, col_out, sems):
    copies = [
        pltpu.make_async_copy(source, target, sems.at[k])
        for k, (source, target) in enumerate(((plan_ref, plan_out), (row_ref, row_out), (col_ref, col_out)))
    ]
    for copy in copies:
        copy.start()
    for copy in copies:
        copy.wait()


def hand_over(*held):
    anywhere = pl.BlockSpec(memory_space=pl.ANY)
    return pl.pallas_call(
        hand_over_kernel,
        out_shape=tuple(jax.ShapeDtypeStruct(value.shape, value.dtype) for value in held),
        in_specs=[pl.BlockSpec(memory_space=pltpu.VMEM)] * len(held),
        out_specs=(anywhere,) * len(held),
        scratch_shapes=[pltpu.SemaphoreType.DMA((len(held),))],
    )(*(pltpu.with_memory_space_constraint(value, pltpu.VMEM) for value in held))


def per_device(peers, teacher_hidden, projection, student_hidden, teacher_segment, student_segment):
    rows, cols, feats = teacher_segment.shape[0], student_segment.shape[0], projection.shape[0]
    depth = teacher_hidden.shape[1]
    chunk = rows // CHUNKS
    vmem = pl.BlockSpec(memory_space=pltpu.VMEM)
    anywhere = pl.BlockSpec(memory_space=pl.ANY)
    plan, row_pot, col_pot = pl.pallas_call(
        functools.partial(kernel, peers),
        out_shape=(
            pltpu.VMEM((rows, cols), jnp.bfloat16),
            pltpu.VMEM((rows,), jnp.float32),
            pltpu.VMEM((cols,), jnp.float32),
        ),
        in_specs=[anywhere] * 3 + [vmem] * 2,
        out_specs=(vmem, vmem, vmem),
        scratch_shapes=[
            pltpu.VMEM((2 * CHUNKS, chunk, depth), jnp.bfloat16),
            pltpu.VMEM((feats, depth), jnp.bfloat16),
            pltpu.VMEM((RING, cols, RING * feats), jnp.bfloat16),
            pltpu.VMEM((CHUNKS, chunk, feats), jnp.float32),
            pltpu.VMEM((2, chunk, feats), jnp.float32),
            pltpu.VMEM((CHUNKS, chunk, feats), jnp.float32),
            pltpu.VMEM((CHUNKS, RING, chunk, RING * feats), jnp.bfloat16),
            pltpu.VMEM((rows, LANES), jnp.float32),
            pltpu.VMEM((rows, LANES), jnp.float32),
            pltpu.VMEM((1, cols), jnp.float32),
            pltpu.VMEM((rows, cols), jnp.float32),
            pltpu.VMEM((rows, LANES), jnp.float32),
            pltpu.VMEM((rows, LANES), jnp.float32),
            pltpu.VMEM((rows, LANES), jnp.float32),
            pltpu.VMEM((CHUNKS, 1, 3 * cols), jnp.float32),
            pltpu.VMEM((CHUNKS, 1, 2 * chunk), jnp.float32),
            pltpu.VMEM((CHUNKS, 2 * REACH + 1, 1, 3 * chunk), jnp.float32),
            pltpu.VMEM((ITERS - 1, 2 * REACH + 1, 1, rows), jnp.float32),
            pltpu.VMEM((peers, 1, rows), jnp.float32),
            pltpu.VMEM((2 * REACH + 1, 1, 3 * cols), jnp.float32),
            pltpu.VMEM((ITERS - 1, 2 * REACH + 1, 1, cols), jnp.float32),
            pltpu.VMEM((peers, 1, 2 * cols), jnp.float32),
            pltpu.SemaphoreType.DMA((2 * CHUNKS,)),
            pltpu.SemaphoreType.DMA((2,)),
            pltpu.SemaphoreType.DMA((CHUNKS,)),
            pltpu.SemaphoreType.DMA((CHUNKS,)),
            pltpu.SemaphoreType.DMA((CHUNKS, 14)),
            pltpu.SemaphoreType.DMA((CHUNKS, 14)),
            pltpu.SemaphoreType.DMA((CHUNKS + 2 * ITERS - 1,)),
            pltpu.SemaphoreType.DMA((CHUNKS + 2 * ITERS - 1,)),
            pltpu.SemaphoreType.DMA((2,)),
            pltpu.SemaphoreType.DMA((2,)),
            pltpu.SemaphoreType.REGULAR((TEA_HALF - 1,)),
        ],
        compiler_params=pltpu.CompilerParams(
            collective_id=1, has_side_effects=True, vmem_limit_bytes=60 * 1024 * 1024
        ),
    )(teacher_hidden, projection, student_hidden, teacher_segment, student_segment)
    return hand_over(plan, row_pot, col_pot)


def solution(mesh):
    placed = (P("tea", "hid"), P("stu", "hid"), P("stu", None), P(("tea", "hid")), P("stu"))
    return jax.shard_map(
        functools.partial(per_device, mesh.shape["stu"]),
        mesh=mesh,
        in_specs=placed,
        out_specs=(P(("tea", "hid"), "stu"), P(("tea", "hid")), P("stu")),
        check_vma=False,
    )
```

```python
import functools

import jax
import jax.numpy as jnp
import numpy as np
from jax import lax
from jax.experimental import pallas as pl
from jax.experimental.pallas import tpu as pltpu
from jax.sharding import PartitionSpec as P

ITERS = 3
INV_EPSILON = float(np.float32(1.0) / np.float32(0.004))
FLOOR = -1e30
SAFE = -1e29
LANES = 128
ROW_BLOCK = 128
CHUNKS = 4
RING = 4
TEA_HALF = 4
REACH = 2
CONTRACT_LAST = (((1,), (1,)), ((), ()))


def to_lanes(part, combine):
    return combine(jnp.transpose(part), axis=0, keepdims=True)


def to_rows(vector):
    count = vector.shape[1]
    return jnp.transpose(jnp.broadcast_to(vector, (LANES, count)))


def merge(slots, width):
    tops, sums, counts = (slots[:, :, k * width:(k + 1) * width] for k in range(3))
    top = jnp.max(tops, axis=0)
    total = jnp.sum(sums * jnp.exp(tops - top), axis=0)
    count = jnp.sum(counts, axis=0)
    return jnp.log(count) - (top + jnp.log(total)), count


def kernel(
    peers,
    teacher_ref, proj_ref, student_ref, tseg_ref, sseg_ref,
    plan_ref, row_out, col_out,
    teacher, proj, student, theirs, mine, incoming, gathered, squares, highest, sinv,
    scaled, left, right, spare, gains, row_pots, row_first, row_next, row_last, col_first, col_next, col_last,
    teacher_sem, weight_sem, core_send, core_recv, ring_send, ring_recv, near_send, near_recv, far_send, far_recv, token,
):
    rows, cols = scaled.shape
    feats = proj.shape[0]
    chunk = rows // CHUNKS
    half = chunk // 2
    blocks = rows // ROW_BLOCK
    strips = [slice(k * LANES, (k + 1) * LANES) for k in range(cols // LANES)]
    cores = 2
    stu = lax.axis_index("stu")
    hid = lax.axis_index("hid")
    place = lax.axis_index("tea") * cores + hid

    y, x = stu // RING, lax.rem(stu, RING)
    major, minor = y + hid * (x - y), x + hid * (y - x)

    def stu_of(big, small):
        return (big + hid * (small - big)) * RING + small + hid * (big - small)

    def around(index, step):
        return lax.rem(index + step + RING, RING)

    def stu_peer(step):
        return {"stu": lax.rem(stu + step + peers, peers)}

    def tea_peer(step):
        other = lax.rem(place + step + peers, peers)
        return {"tea": other // cores, "hid": lax.rem(other, cores)}

    def beside(side):
        other = lax.rem(place + 2 * side + peers, peers) // cores
        return {"tea": other, "hid": 1 - hid}

    def pass_token(k):
        for side in (1, -1):
            pl.semaphore_signal(token.at[k], inc=1, device_id=tea_peer(2 * side))

    def teacher_copy(c, whose):
        start = pl.multiple_of((whose * CHUNKS + c) * chunk, chunk)
        return pltpu.make_async_copy(
            teacher_ref.at[pl.ds(start, chunk)], teacher.at[whose * CHUNKS + c], teacher_sem.at[whose * CHUNKS + c]
        )

    proj_copy = pltpu.make_async_copy(proj_ref, proj, weight_sem.at[0])
    proj_copy.start()

    @pl.loop(0, CHUNKS)
    def _(c):
        teacher_copy(c, 1 - hid).start()
        teacher_copy(c, hid).start()

    @pl.loop(0, peers)
    def _(slot):
        big, small = slot // RING, lax.rem(slot, RING)
        source = pl.multiple_of(stu_of(big, small) * feats, feats)
        target = pl.multiple_of(small * feats, feats)
        pltpu.make_async_copy(
            student_ref.at[:, pl.ds(source, feats)], student.at[big, :, pl.ds(target, feats)], weight_sem.at[1]
        ).start()

    sseg = sseg_ref[...].reshape(1, cols).astype(jnp.float32)
    barrier = pltpu.get_barrier_semaphore()

    for side in (1, -1):
        pl.semaphore_signal(barrier, inc=1, device_id={"stu": stu_of(major, around(minor, side))})
        pl.semaphore_signal(barrier, inc=1, device_id={"stu": stu_of(around(major, side), minor)})
        pl.semaphore_signal(barrier, inc=1, device_id=tea_peer(2 * side))
        pl.semaphore_signal(barrier, inc=1, device_id=beside(side))
    pl.semaphore_signal(barrier, inc=1, device_id={"hid": 1 - hid})

    proj_copy.wait()

    def project(c, whose):
        teacher_copy(c, whose).wait()
        return lax.dot_general(
            teacher[whose * CHUNKS + c], proj[...], CONTRACT_LAST, preferred_element_type=jnp.float32
        )

    def core_copy(c):
        return pltpu.make_async_remote_copy(
            src_ref=theirs.at[c], dst_ref=incoming.at[c],
            send_sem=core_send.at[c], recv_sem=core_recv.at[c], device_id={"hid": 1 - hid},
        )

    def ring_copy(c, stage, ref, big, small):
        return pltpu.make_async_remote_copy(
            src_ref=ref, dst_ref=ref,
            send_sem=ring_send.at[c, stage], recv_sem=ring_recv.at[c, stage],
            device_id={"stu": stu_of(around(big, 0), around(small, 0))},
        )

    def block(c, big, small, part=slice(None)):
        return gathered.at[c, around(big, 0), part, pl.ds(pl.multiple_of(around(small, 0) * feats, feats), feats)]

    def bundle(c, big, part=slice(None)):
        return gathered.at[c, around(big, 0), part]

    low, high = pl.ds(0, half), pl.ds(half, half)
    offsets = (0, -1, 1, 2)

    def along_minor(c, k, side, small, part=slice(None)):
        return ring_copy(c, k, block(c, major, small, part), major, minor + side)

    def along_major(c, which, side, big):
        return ring_copy(
            c, 4 + 2 * which + (side < 0), block(c, big, minor + offsets[which]), major + side, minor
        )

    def relay(c, side, big):
        return ring_copy(c, 12 + (side < 0), bundle(c, big, low if side > 0 else high), major + side, minor)

    def send_major(c, which):
        along_major(c, which, 1, major).start()
        along_major(c, which, -1, major).start()

    def own_stage(c):
        along_minor(c, 0, 1, minor).start()
        along_minor(c, 1, -1, minor).start()
        send_major(c, 0)

    def near_stage(c):
        along_minor(c, 0, 1, minor - 1).wait_recv()
        along_minor(c, 2, 1, minor - 1, low).start()
        send_major(c, 1)
        along_minor(c, 1, -1, minor + 1).wait_recv()
        along_minor(c, 3, -1, minor + 1, high).start()
        send_major(c, 2)

    def far_stage(c):
        along_minor(c, 2, 1, minor + 2, low).wait_recv()
        along_minor(c, 3, -1, minor + 2, high).wait_recv()
        send_major(c, 3)

    def relay_stage(c):
        for side in (1, -1):
            for which in range(4):
                along_major(c, which, side, major - side).wait_recv()
            relay(c, side, major - side).start()

    def last_stage(c):
        relay(c, 1, major + 2).wait_recv()
        relay(c, -1, major + 2).wait_recv()

    def sent(c):
        along_minor(c, 0, 1, minor).wait_send()
        along_minor(c, 1, -1, minor).wait_send()
        along_minor(c, 2, 1, minor - 1, low).wait_send()
        along_minor(c, 3, -1, minor + 1, high).wait_send()
        for side in (1, -1):
            for which in range(4):
                along_major(c, which, side, major).wait_send()
            relay(c, side, major - side).wait_send()

    def by_block(body, init=None, first=0, count=blocks):
        def step(b, carry):
            return body(pl.ds(pl.multiple_of(b * ROW_BLOCK, ROW_BLOCK), ROW_BLOCK), carry)
        return lax.fori_loop(first, first + count, step, init)

    def student_norms():
        pltpu.make_async_copy(student, student, weight_sem.at[1]).wait()

        @pl.loop(0, cols // LANES)
        def _(k):
            at = pl.ds(pl.multiple_of(k * LANES, LANES), LANES)
            def add(big, total):
                for j in range(RING * feats // LANES):
                    value = student[big, at, j * LANES:(j + 1) * LANES].astype(jnp.float32)
                    total += value * value
                return total
            total = lax.fori_loop(0, RING, add, jnp.zeros((LANES, LANES), jnp.float32))
            sinv[:, at] = lax.rsqrt(to_lanes(total, jnp.sum) + 1e-06)

    def first_rows(at, carry):
        tinv = lax.rsqrt(jnp.sum(squares[at, :], axis=1, keepdims=True) + 1e-06)
        tseg = left[at, :]
        tops = jnp.full((ROW_BLOCK, LANES), SAFE, jnp.float32)
        for strip in strips:
            support = tseg == sseg[:, strip]
            value = (scaled[at, strip] * tinv * sinv[:, strip] - 1.0) * INV_EPSILON
            value = jnp.where(support, value, FLOOR)
            scaled[at, strip] = value
            tops = jnp.maximum(tops, value)
        top = jnp.max(tops, axis=1, keepdims=True)
        total = jnp.zeros((ROW_BLOCK, LANES), jnp.float32)
        for strip in strips:
            total += jnp.exp(scaled[at, strip] - top)
        highest[at, :] = jnp.broadcast_to(top, (ROW_BLOCK, LANES))
        right[at, :] = total
        return carry

    def count_rows(at, carry):
        tseg = left[at, :]
        count = jnp.zeros((ROW_BLOCK, LANES), jnp.float32)
        for strip in strips:
            count += jnp.where(tseg == sseg[:, strip], 1.0, 0.0)
        spare[at, :] = count
        return carry

    def rows_of(c):
        return pl.ds(pl.multiple_of(c * chunk, chunk), chunk)

    def product(c, big):
        return lax.dot_general(
            gathered[c, big], student[big], CONTRACT_LAST, preferred_element_type=jnp.float32
        )

    def squared(c, big, total):
        for j in range(RING * feats // LANES):
            value = gathered[c, big, :, j * LANES:(j + 1) * LANES].astype(jnp.float32)
            total += value * value
        return total

    @pl.loop(0, CHUNKS + 4)
    def _(slot):
        def due(stage):
            return (slot >= stage) & (slot < CHUNKS + stage)

        @pl.when(due(0))
        def _():
            theirs[slot] = project(slot, 1 - hid)

        @pl.when(slot == 0)
        def _():
            pl.semaphore_wait(barrier, 9)
            pass_token(0)

        @pl.when(due(0))
        def _():
            core_copy(slot).start()

        @pl.when(due(1))
        def _():
            c = slot - 1
            core_copy(c).wait_recv()
            block(c, major, minor)[...] = (mine[lax.rem(c, 2)] + incoming[c]).astype(jnp.bfloat16)
            own_stage(c)

        @pl.when(due(0))
        def _():
            mine[lax.rem(slot, 2)] = project(slot, hid)

        @pl.when(due(3))
        def _():
            near_stage(slot - 3)

        @pl.when(due(4))
        def _():
            far_stage(slot - 4)

    left[...] = to_rows(tseg_ref[...].reshape(1, rows).astype(jnp.float32))
    student_norms()
    for k in range(1, TEA_HALF):
        pl.semaphore_wait(token.at[k - 1], 2)
        if k < TEA_HALF - 1:
            pass_token(k)

    @pl.loop(0, CHUNKS)
    def _(c):
        relay_stage(c)
        at = rows_of(c)
        before, after = around(major, -1), around(major, 1)
        scaled[at, :] = product(c, major) + product(c, before) + product(c, after)
        total = squared(c, major, jnp.zeros((chunk, LANES), jnp.float32))
        squares[at, :] = squared(c, after, squared(c, before, total))
        by_block(count_rows, None, c * (chunk // ROW_BLOCK), chunk // ROW_BLOCK)
        row_first[c, REACH, :, 2 * chunk:] = to_lanes(spare[at, :], jnp.sum)

    def near_copy(slots, peer, phase, step):
        return pltpu.make_async_remote_copy(
            src_ref=slots.at[REACH], dst_ref=slots.at[REACH - step],
            send_sem=near_send.at[phase], recv_sem=near_recv.at[phase], device_id=peer(step),
        )

    def near_start(slots, peer, phase):
        for step in (-2, 2, -1, 1):
            near_copy(slots, peer, phase, step).start()

    def near_all(slots, peer, phase):
        whole = slots.at[pl.ds(0, 2 * REACH)]
        return pltpu.make_async_remote_copy(
            src_ref=whole, dst_ref=whole,
            send_sem=near_send.at[phase], recv_sem=near_recv.at[phase], device_id=peer(1),
        )

    def spread_copy(ref, peer, phase, step, sends=far_send, recvs=far_recv):
        return pltpu.make_async_remote_copy(
            src_ref=ref, dst_ref=ref, send_sem=sends.at[phase], recv_sem=recvs.at[phase], device_id=peer(step)
        )

    def row_phase(step):
        return CHUNKS + step - 1

    def col_phase(step):
        return CHUNKS + ITERS - 1 + step

    def fold(values):
        return jnp.sum(values.reshape(-1, 8, LANES), axis=0)

    def block_of(c, init, body):
        return by_block(body, init, c * (chunk // ROW_BLOCK), chunk // ROW_BLOCK)

    blank = jnp.zeros((8, LANES), jnp.float32)
    lowest = jnp.full((8, LANES), SAFE, jnp.float32)

    def complete(c):
        last_stage(c)
        at = rows_of(c)
        opposite = around(major, 2)
        scaled[at, :] += product(c, opposite)
        squares[at, :] = squared(c, opposite, squares[at, :])
        block_of(c, None, first_rows)
        row_first[c, REACH] = jnp.concatenate(
            [
                to_lanes(highest[at, :], jnp.max),
                to_lanes(right[at, :], jnp.sum),
                row_first[c, REACH, :, 2 * chunk:],
            ],
            axis=1,
        )
        near_start(row_first.at[c], stu_peer, c)

    def held_rows(c):
        return row_first[c, REACH, :, 2 * chunk:] > 0.0

    def first_columns(c):
        near_all(row_first.at[c], stu_peer, c).wait_recv()
        pot, count = merge(row_first[c], chunk)
        pot = jnp.where(held_rows(c), pot, 0.0)
        row_pots[c] = jnp.concatenate([pot, count], axis=1)
        left[rows_of(c), :] = to_rows(pot)

        def largest(at, tops):
            pot = left[at, :]
            new = []
            for strip, top in zip(strips, tops):
                value = scaled[at, strip] + pot
                new.append(jnp.maximum(top, jnp.max(value.reshape(-1, 8, LANES), axis=0)))
            return new

        tops = [jnp.max(top, axis=0, keepdims=True) for top in block_of(c, [lowest] * len(strips), largest)]

        def terms(at, carry):
            pot = left[at, :]
            new = []
            for strip, top, (total, count) in zip(strips, tops, carry):
                value = scaled[at, strip] + pot
                term = jnp.exp(value - top)
                scaled[at, strip] = term
                new.append((total + fold(term), count + fold(jnp.where(value > SAFE, 1.0, 0.0))))
            return new

        sums = block_of(c, [(blank, blank)] * len(strips), terms)
        flat = [jnp.sum(value, axis=0, keepdims=True) for k in range(2) for value in [pair[k] for pair in sums]]
        gains[c] = jnp.concatenate(tops + flat, axis=1)

    @pl.loop(0, CHUNKS + 1)
    def _(slot):
        @pl.when(slot < CHUNKS)
        def _():
            complete(slot)

        @pl.when(slot > 0)
        def _():
            first_columns(slot - 1)

    parts = gains[...]
    local_top = jnp.max(parts[:, :, :cols], axis=0)
    local_sum = jnp.sum(parts[:, :, cols:2 * cols] * jnp.exp(parts[:, :, :cols] - local_top), axis=0)
    own_count = jnp.sum(parts[:, :, 2 * cols:], axis=0)
    col_held = own_count > 0.0
    col_first[REACH] = jnp.concatenate([local_top, local_sum, own_count], axis=1)
    near_start(col_first, tea_peer, col_phase(0))

    @pl.loop(0, CHUNKS)
    def _(c):
        near_all(row_first.at[c], stu_peer, c).wait_send()
        core_copy(c).wait_send()
        sent(c)

    near_all(col_first, tea_peer, col_phase(0)).wait_recv()
    col_pot, col_count = merge(col_first[...], cols)
    col_pot = jnp.where(col_held, col_pot, 0.0)
    for c in range(CHUNKS):
        gains[c, :, :cols] = jnp.exp(gains[c, :, :cols] + col_pot)

    def by_chunk_block(body, init=None):
        def step(b, carry):
            at = pl.ds(pl.multiple_of(b * ROW_BLOCK, ROW_BLOCK), ROW_BLOCK)
            return body(at, gains.at[b // (chunk // ROW_BLOCK)], carry)
        return lax.fori_loop(0, blocks, step, init)

    def across(pick):
        return jnp.concatenate([pick(c) for c in range(CHUNKS)], axis=1)

    row_held = across(held_rows)
    first_pot = across(lambda c: row_pots[c, :, :chunk])
    row_count = across(lambda c: row_pots[c, :, chunk:])

    for step in range(1, ITERS):
        last = step == ITERS - 1
        row_slots, col_slots = row_next.at[step - 1], col_next.at[step - 1]

        def later_rows(at, gain, carry):
            total = scaled[at, strips[0]] * gain[:, strips[0]]
            for strip in strips[1:]:
                total += scaled[at, strip] * gain[:, strip]
            right[at, :] = total
            return carry

        by_chunk_block(later_rows)
        row_slots[REACH] = to_lanes(right[...], jnp.sum)
        near_start(row_slots, stu_peer, row_phase(step))
        near_all(row_slots, stu_peer, row_phase(step)).wait_recv()
        factor = row_count / jnp.sum(row_slots[...], axis=0)
        left[...] = to_rows(jnp.where(row_held, factor, 0.0))

        def later_cols(at, gain, sums):
            factor = left[at, :]
            return [
                value + fold(scaled[at, strip] * factor) * gain[:, strip] for strip, value in zip(strips, sums)
            ]

        sums = by_chunk_block(later_cols, [blank] * len(strips))
        total = jnp.concatenate([jnp.sum(value, axis=0, keepdims=True) for value in sums], axis=1)
        if last:
            base = jnp.where(col_held, -col_pot - jnp.log(col_count), SAFE)
            col_last[place] = jnp.concatenate([base, total], axis=1)
            for k in (-2, 2, -1, 1):
                spread_copy(col_last.at[place], tea_peer, col_phase(step), k, near_send, near_recv).start()

            @pl.loop(REACH + 1, peers - REACH)
            def _(k):
                spread_copy(col_last.at[place], tea_peer, 1, k).start()

            row_last[stu] = jnp.where(row_held, first_pot + jnp.log(factor), FLOOR)

            @pl.loop(1, peers)
            def _(k):
                spread_copy(row_last.at[stu], stu_peer, 0, k).start()

            near_cols = spread_copy(
                col_last.at[pl.ds(0, 2 * REACH)], tea_peer, col_phase(step), 1, near_send, near_recv
            )
            near_cols.wait_recv()
            for k in (-2, -1, 1, 2):
                total += col_last[lax.rem(place + k + peers, peers), :, cols:]
        else:
            col_slots[REACH] = total
            near_start(col_slots, tea_peer, col_phase(step))
            near_all(col_slots, tea_peer, col_phase(step)).wait_recv()
            total = jnp.sum(col_slots[...], axis=0)
        fresh = jnp.where(col_held, col_count / total, 1.0)
        col_pot = col_pot + jnp.log(fresh)
        for c in range(CHUNKS):
            gains[c, :, :cols] = gains[c, :, :cols] * fresh

    def finish(at, gain, carry):
        factor = left[at, :]
        for strip in strips:
            plan_ref[at, strip] = (scaled[at, strip] * factor * gain[:, strip]).astype(jnp.bfloat16)
        return carry

    by_chunk_block(finish)
    far_rows = spread_copy(row_last.at[pl.ds(0, peers - 1)], stu_peer, 0, 1)
    far_cols = spread_copy(col_last.at[pl.ds(0, peers - 1 - 2 * REACH)], tea_peer, 1, 1)
    near_cols.wait_send()
    near_all(col_first, tea_peer, col_phase(0)).wait_send()
    for step in range(1, ITERS):
        near_all(row_next.at[step - 1], stu_peer, row_phase(step)).wait_send()
    for step in range(1, ITERS - 1):
        near_all(col_next.at[step - 1], tea_peer, col_phase(step)).wait_send()
    far_rows.wait_recv()
    row_out[...] = jnp.max(row_last[...], axis=0).reshape(rows)
    far_cols.wait_recv()
    base, total = col_last[:, :, :cols], col_last[:, :, cols:]
    top = jnp.max(base, axis=0)
    col_out[...] = -(top + jnp.log(jnp.sum(total * jnp.exp(base - top), axis=0))).reshape(cols)

    far_rows.wait_send()
    far_cols.wait_send()

def hand_over_kernel(plan_ref, row_ref, col_ref, plan_out, row_out, col_out, sems):
    copies = [
        pltpu.make_async_copy(source, target, sems.at[k])
        for k, (source, target) in enumerate(((plan_ref, plan_out), (row_ref, row_out), (col_ref, col_out)))
    ]
    for copy in copies:
        copy.start()
    for copy in copies:
        copy.wait()


def hand_over(*held):
    anywhere = pl.BlockSpec(memory_space=pl.ANY)
    return pl.pallas_call(
        hand_over_kernel,
        out_shape=tuple(jax.ShapeDtypeStruct(value.shape, value.dtype) for value in held),
        in_specs=[pl.BlockSpec(memory_space=pltpu.VMEM)] * len(held),
        out_specs=(anywhere,) * len(held),
        scratch_shapes=[pltpu.SemaphoreType.DMA((len(held),))],
    )(*(pltpu.with_memory_space_constraint(value, pltpu.VMEM) for value in held))


def per_device(peers, teacher_hidden, projection, student_hidden, teacher_segment, student_segment):
    rows, cols, feats = teacher_segment.shape[0], student_segment.shape[0], projection.shape[0]
    depth = teacher_hidden.shape[1]
    chunk = rows // CHUNKS
    vmem = pl.BlockSpec(memory_space=pltpu.VMEM)
    anywhere = pl.BlockSpec(memory_space=pl.ANY)
    plan, row_pot, col_pot = pl.pallas_call(
        functools.partial(kernel, peers),
        out_shape=(
            pltpu.VMEM((rows, cols), jnp.bfloat16),
            pltpu.VMEM((rows,), jnp.float32),
            pltpu.VMEM((cols,), jnp.float32),
        ),
        in_specs=[anywhere] * 3 + [vmem] * 2,
        out_specs=(vmem, vmem, vmem),
        scratch_shapes=[
            pltpu.VMEM((2 * CHUNKS, chunk, depth), jnp.bfloat16),
            pltpu.VMEM((feats, depth), jnp.bfloat16),
            pltpu.VMEM((RING, cols, RING * feats), jnp.bfloat16),
            pltpu.VMEM((CHUNKS, chunk, feats), jnp.float32),
            pltpu.VMEM((2, chunk, feats), jnp.float32),
            pltpu.VMEM((CHUNKS, chunk, feats), jnp.float32),
            pltpu.VMEM((CHUNKS, RING, chunk, RING * feats), jnp.bfloat16),
            pltpu.VMEM((rows, LANES), jnp.float32),
            pltpu.VMEM((rows, LANES), jnp.float32),
            pltpu.VMEM((1, cols), jnp.float32),
            pltpu.VMEM((rows, cols), jnp.float32),
            pltpu.VMEM((rows, LANES), jnp.float32),
            pltpu.VMEM((rows, LANES), jnp.float32),
            pltpu.VMEM((rows, LANES), jnp.float32),
            pltpu.VMEM((CHUNKS, 1, 3 * cols), jnp.float32),
            pltpu.VMEM((CHUNKS, 1, 2 * chunk), jnp.float32),
            pltpu.VMEM((CHUNKS, 2 * REACH + 1, 1, 3 * chunk), jnp.float32),
            pltpu.VMEM((ITERS - 1, 2 * REACH + 1, 1, rows), jnp.float32),
            pltpu.VMEM((peers, 1, rows), jnp.float32),
            pltpu.VMEM((2 * REACH + 1, 1, 3 * cols), jnp.float32),
            pltpu.VMEM((ITERS - 1, 2 * REACH + 1, 1, cols), jnp.float32),
            pltpu.VMEM((peers, 1, 2 * cols), jnp.float32),
            pltpu.SemaphoreType.DMA((2 * CHUNKS,)),
            pltpu.SemaphoreType.DMA((2,)),
            pltpu.SemaphoreType.DMA((CHUNKS,)),
            pltpu.SemaphoreType.DMA((CHUNKS,)),
            pltpu.SemaphoreType.DMA((CHUNKS, 14)),
            pltpu.SemaphoreType.DMA((CHUNKS, 14)),
            pltpu.SemaphoreType.DMA((CHUNKS + 2 * ITERS - 1,)),
            pltpu.SemaphoreType.DMA((CHUNKS + 2 * ITERS - 1,)),
            pltpu.SemaphoreType.DMA((2,)),
            pltpu.SemaphoreType.DMA((2,)),
            pltpu.SemaphoreType.REGULAR((TEA_HALF - 1,)),
        ],
        compiler_params=pltpu.CompilerParams(
            collective_id=1, has_side_effects=True, vmem_limit_bytes=60 * 1024 * 1024
        ),
    )(teacher_hidden, projection, student_hidden, teacher_segment, student_segment)
    return hand_over(plan, row_pot, col_pot)


def solution(mesh):
    placed = (P("tea", "hid"), P("stu", "hid"), P("stu", None), P(("tea", "hid")), P("stu"))
    return jax.shard_map(
        functools.partial(per_device, mesh.shape["stu"]),
        mesh=mesh,
        in_specs=placed,
        out_specs=(P(("tea", "hid"), "stu"), P(("tea", "hid")), P("stu")),
        check_vma=False,
    )
```

```python
import functools

import jax
import jax.numpy as jnp
import numpy as np
from jax import lax
from jax.experimental import pallas as pl
from jax.experimental.pallas import tpu as pltpu
from jax.sharding import PartitionSpec as P

ITERS = 3
INV_EPSILON = float(np.float32(1.0) / np.float32(0.004))
FLOOR = -1e30
SAFE = -1e29
LANES = 128
ROW_BLOCK = 128
CHUNKS = 4
RING = 4
TEA_HALF = 4
REACH = 2
CONTRACT_LAST = (((1,), (1,)), ((), ()))


def to_lanes(part, combine):
    return combine(jnp.transpose(part), axis=0, keepdims=True)


def to_rows(vector):
    count = vector.shape[1]
    return jnp.transpose(jnp.broadcast_to(vector, (LANES, count)))


def merge(slots, width):
    tops, sums, counts = (slots[:, :, k * width:(k + 1) * width] for k in range(3))
    top = jnp.max(tops, axis=0)
    total = jnp.sum(sums * jnp.exp(tops - top), axis=0)
    count = jnp.sum(counts, axis=0)
    return jnp.log(count) - (top + jnp.log(total)), count


def kernel(
    peers,
    teacher_ref, proj_ref, student_ref, tseg_ref, sseg_ref,
    plan_ref, row_out, col_out,
    teacher, proj, student, theirs, mine, incoming, gathered, squares, highest, sinv,
    scaled, left, right, spare, gains, row_pots, row_first, row_next, row_last, col_first, col_next, col_last,
    teacher_sem, weight_sem, core_send, core_recv, ring_send, ring_recv, near_send, near_recv, far_send, far_recv, token,
):
    rows, cols = scaled.shape
    feats = proj.shape[0]
    chunk = rows // CHUNKS
    half = chunk // 2
    blocks = rows // ROW_BLOCK
    strips = [slice(k * LANES, (k + 1) * LANES) for k in range(cols // LANES)]
    cores = 2
    stu = lax.axis_index("stu")
    hid = lax.axis_index("hid")
    place = lax.axis_index("tea") * cores + hid

    y, x = stu // RING, lax.rem(stu, RING)
    major, minor = y + hid * (x - y), x + hid * (y - x)

    def stu_of(big, small):
        return (big + hid * (small - big)) * RING + small + hid * (big - small)

    def around(index, step):
        return lax.rem(index + step + RING, RING)

    def stu_peer(step):
        return {"stu": lax.rem(stu + step + peers, peers)}

    def tea_peer(step):
        other = lax.rem(place + step + peers, peers)
        return {"tea": other // cores, "hid": lax.rem(other, cores)}

    def beside(side):
        other = lax.rem(place + 2 * side + peers, peers) // cores
        return {"tea": other, "hid": 1 - hid}

    def pass_token(k):
        for side in (1, -1):
            pl.semaphore_signal(token.at[k], inc=1, device_id=tea_peer(2 * side))

    def teacher_copy(c, whose):
        start = pl.multiple_of((whose * CHUNKS + c) * chunk, chunk)
        return pltpu.make_async_copy(
            teacher_ref.at[pl.ds(start, chunk)], teacher.at[whose * CHUNKS + c], teacher_sem.at[whose * CHUNKS + c]
        )

    proj_copy = pltpu.make_async_copy(proj_ref, proj, weight_sem.at[0])
    proj_copy.start()

    @pl.loop(0, CHUNKS)
    def _(c):
        teacher_copy(c, 1 - hid).start()
        teacher_copy(c, hid).start()

    @pl.loop(0, peers)
    def _(slot):
        big, small = slot // RING, lax.rem(slot, RING)
        source = pl.multiple_of(stu_of(big, small) * feats, feats)
        target = pl.multiple_of(small * feats, feats)
        pltpu.make_async_copy(
            student_ref.at[:, pl.ds(source, feats)], student.at[big, :, pl.ds(target, feats)], weight_sem.at[1]
        ).start()

    sseg = sseg_ref[...].reshape(1, cols).astype(jnp.float32)
    barrier = pltpu.get_barrier_semaphore()

    for side in (1, -1):
        pl.semaphore_signal(barrier, inc=1, device_id={"stu": stu_of(major, around(minor, side))})
        pl.semaphore_signal(barrier, inc=1, device_id={"stu": stu_of(around(major, side), minor)})
        pl.semaphore_signal(barrier, inc=1, device_id=tea_peer(2 * side))
        pl.semaphore_signal(barrier, inc=1, device_id=beside(side))
    pl.semaphore_signal(barrier, inc=1, device_id={"hid": 1 - hid})

    proj_copy.wait()

    def project(c, whose):
        teacher_copy(c, whose).wait()
        return lax.dot_general(
            teacher[whose * CHUNKS + c], proj[...], CONTRACT_LAST, preferred_element_type=jnp.float32
        )

    def core_copy(c):
        return pltpu.make_async_remote_copy(
            src_ref=theirs.at[c], dst_ref=incoming.at[c],
            send_sem=core_send.at[c], recv_sem=core_recv.at[c], device_id={"hid": 1 - hid},
        )

    def ring_copy(c, stage, ref, big, small):
        return pltpu.make_async_remote_copy(
            src_ref=ref, dst_ref=ref,
            send_sem=ring_send.at[c, stage], recv_sem=ring_recv.at[c, stage],
            device_id={"stu": stu_of(around(big, 0), around(small, 0))},
        )

    def block(c, big, small, part=slice(None)):
        return gathered.at[c, around(big, 0), part, pl.ds(pl.multiple_of(around(small, 0) * feats, feats), feats)]

    def bundle(c, big, part=slice(None)):
        return gathered.at[c, around(big, 0), part]

    low, high = pl.ds(0, half), pl.ds(half, half)
    offsets = (0, -1, 1, 2)

    def along_minor(c, k, side, small, part=slice(None)):
        return ring_copy(c, k, block(c, major, small, part), major, minor + side)

    def along_major(c, which, side, big):
        return ring_copy(
            c, 4 + 2 * which + (side < 0), block(c, big, minor + offsets[which]), major + side, minor
        )

    def relay(c, side, big):
        return ring_copy(c, 12 + (side < 0), bundle(c, big, low if side > 0 else high), major + side, minor)

    def send_major(c, which):
        along_major(c, which, 1, major).start()
        along_major(c, which, -1, major).start()

    def own_stage(c):
        along_minor(c, 0, 1, minor).start()
        along_minor(c, 1, -1, minor).start()
        send_major(c, 0)

    def near_stage(c):
        along_minor(c, 0, 1, minor - 1).wait_recv()
        along_minor(c, 2, 1, minor - 1, low).start()
        send_major(c, 1)
        along_minor(c, 1, -1, minor + 1).wait_recv()
        along_minor(c, 3, -1, minor + 1, high).start()
        send_major(c, 2)

    def far_stage(c):
        along_minor(c, 2, 1, minor + 2, low).wait_recv()
        along_minor(c, 3, -1, minor + 2, high).wait_recv()
        send_major(c, 3)

    def relay_stage(c):
        for side in (1, -1):
            for which in range(4):
                along_major(c, which, side, major - side).wait_recv()
            relay(c, side, major - side).start()

    def last_stage(c):
        relay(c, 1, major + 2).wait_recv()
        relay(c, -1, major + 2).wait_recv()

    def sent(c):
        along_minor(c, 0, 1, minor).wait_send()
        along_minor(c, 1, -1, minor).wait_send()
        along_minor(c, 2, 1, minor - 1, low).wait_send()
        along_minor(c, 3, -1, minor + 1, high).wait_send()
        for side in (1, -1):
            for which in range(4):
                along_major(c, which, side, major).wait_send()
            relay(c, side, major - side).wait_send()

    def by_block(body, init=None, first=0, count=blocks):
        def step(b, carry):
            return body(pl.ds(pl.multiple_of(b * ROW_BLOCK, ROW_BLOCK), ROW_BLOCK), carry)
        return lax.fori_loop(first, first + count, step, init)

    def student_norms():
        pltpu.make_async_copy(student, student, weight_sem.at[1]).wait()

        @pl.loop(0, cols // LANES)
        def _(k):
            at = pl.ds(pl.multiple_of(k * LANES, LANES), LANES)
            def add(big, total):
                for j in range(RING * feats // LANES):
                    value = student[big, at, j * LANES:(j + 1) * LANES].astype(jnp.float32)
                    total += value * value
                return total
            total = lax.fori_loop(0, RING, add, jnp.zeros((LANES, LANES), jnp.float32))
            sinv[:, at] = lax.rsqrt(to_lanes(total, jnp.sum) + 1e-06)

    def first_rows(at, carry):
        tinv = lax.rsqrt(jnp.sum(squares[at, :], axis=1, keepdims=True) + 1e-06)
        tseg = left[at, :]
        tops = jnp.full((ROW_BLOCK, LANES), SAFE, jnp.float32)
        for strip in strips:
            support = tseg == sseg[:, strip]
            value = (scaled[at, strip] * tinv * sinv[:, strip] - 1.0) * INV_EPSILON
            value = jnp.where(support, value, FLOOR)
            scaled[at, strip] = value
            tops = jnp.maximum(tops, value)
        top = jnp.max(tops, axis=1, keepdims=True)
        total = jnp.zeros((ROW_BLOCK, LANES), jnp.float32)
        for strip in strips:
            total += jnp.exp(scaled[at, strip] - top)
        highest[at, :] = jnp.broadcast_to(top, (ROW_BLOCK, LANES))
        right[at, :] = total
        return carry

    def count_rows(at, carry):
        tseg = left[at, :]
        count = jnp.zeros((ROW_BLOCK, LANES), jnp.float32)
        for strip in strips:
            count += jnp.where(tseg == sseg[:, strip], 1.0, 0.0)
        spare[at, :] = count
        return carry

    def rows_of(c):
        return pl.ds(pl.multiple_of(c * chunk, chunk), chunk)

    def product(c, big):
        return lax.dot_general(
            gathered[c, big], student[big], CONTRACT_LAST, preferred_element_type=jnp.float32
        )

    def squared(c, big, total):
        for j in range(RING * feats // LANES):
            value = gathered[c, big, :, j * LANES:(j + 1) * LANES].astype(jnp.float32)
            total += value * value
        return total

    @pl.loop(0, CHUNKS + 4)
    def _(slot):
        def due(stage):
            return (slot >= stage) & (slot < CHUNKS + stage)

        @pl.when(due(0))
        def _():
            theirs[slot] = project(slot, 1 - hid)

        @pl.when(slot == 0)
        def _():
            left[...] = to_rows(tseg_ref[...].reshape(1, rows).astype(jnp.float32))
            pl.semaphore_wait(barrier, 9)
            pass_token(0)

        @pl.when(due(0))
        def _():
            core_copy(slot).start()

        @pl.when(due(1))
        def _():
            c = slot - 1
            core_copy(c).wait_recv()
            block(c, major, minor)[...] = (mine[lax.rem(c, 2)] + incoming[c]).astype(jnp.bfloat16)
            own_stage(c)

        @pl.when(due(0))
        def _():
            mine[lax.rem(slot, 2)] = project(slot, hid)

        @pl.when(due(3))
        def _():
            near_stage(slot - 3)

        @pl.when(due(4))
        def _():
            far_stage(slot - 4)

    student_norms()
    for k in range(1, TEA_HALF):
        pl.semaphore_wait(token.at[k - 1], 2)
        if k < TEA_HALF - 1:
            pass_token(k)

    @pl.loop(0, CHUNKS)
    def _(c):
        relay_stage(c)
        at = rows_of(c)
        before, after = around(major, -1), around(major, 1)
        scaled[at, :] = product(c, major) + product(c, before) + product(c, after)
        total = squared(c, major, jnp.zeros((chunk, LANES), jnp.float32))
        squares[at, :] = squared(c, after, squared(c, before, total))
        by_block(count_rows, None, c * (chunk // ROW_BLOCK), chunk // ROW_BLOCK)
        row_first[c, REACH, :, 2 * chunk:] = to_lanes(spare[at, :], jnp.sum)

    def near_copy(slots, peer, phase, step):
        return pltpu.make_async_remote_copy(
            src_ref=slots.at[REACH], dst_ref=slots.at[REACH - step],
            send_sem=near_send.at[phase], recv_sem=near_recv.at[phase], device_id=peer(step),
        )

    def near_start(slots, peer, phase):
        for step in (-2, 2, -1, 1):
            near_copy(slots, peer, phase, step).start()

    def near_all(slots, peer, phase):
        whole = slots.at[pl.ds(0, 2 * REACH)]
        return pltpu.make_async_remote_copy(
            src_ref=whole, dst_ref=whole,
            send_sem=near_send.at[phase], recv_sem=near_recv.at[phase], device_id=peer(1),
        )

    def spread_copy(ref, peer, phase, step, sends=far_send, recvs=far_recv):
        return pltpu.make_async_remote_copy(
            src_ref=ref, dst_ref=ref, send_sem=sends.at[phase], recv_sem=recvs.at[phase], device_id=peer(step)
        )

    def row_phase(step):
        return CHUNKS + step - 1

    def col_phase(step):
        return CHUNKS + ITERS - 1 + step

    def fold(values):
        return jnp.sum(values.reshape(-1, 8, LANES), axis=0)

    def block_of(c, init, body):
        return by_block(body, init, c * (chunk // ROW_BLOCK), chunk // ROW_BLOCK)

    blank = jnp.zeros((8, LANES), jnp.float32)
    lowest = jnp.full((8, LANES), SAFE, jnp.float32)

    def complete(c):
        last_stage(c)
        at = rows_of(c)
        opposite = around(major, 2)
        scaled[at, :] += product(c, opposite)
        squares[at, :] = squared(c, opposite, squares[at, :])
        block_of(c, None, first_rows)
        row_first[c, REACH] = jnp.concatenate(
            [
                to_lanes(highest[at, :], jnp.max),
                to_lanes(right[at, :], jnp.sum),
                row_first[c, REACH, :, 2 * chunk:],
            ],
            axis=1,
        )
        near_start(row_first.at[c], stu_peer, c)

    def held_rows(c):
        return row_first[c, REACH, :, 2 * chunk:] > 0.0

    def first_columns(c):
        near_all(row_first.at[c], stu_peer, c).wait_recv()
        pot, count = merge(row_first[c], chunk)
        pot = jnp.where(held_rows(c), pot, 0.0)
        row_pots[c] = jnp.concatenate([pot, count], axis=1)
        left[rows_of(c), :] = to_rows(pot)

        def largest(at, tops):
            pot = left[at, :]
            new = []
            for strip, top in zip(strips, tops):
                value = scaled[at, strip] + pot
                scaled[at, strip] = value
                new.append(jnp.maximum(top, jnp.max(value.reshape(-1, 8, LANES), axis=0)))
            return new

        tops = [jnp.max(top, axis=0, keepdims=True) for top in block_of(c, [lowest] * len(strips), largest)]

        def terms(at, carry):
            new = []
            for strip, top, (total, count) in zip(strips, tops, carry):
                value = scaled[at, strip]
                term = jnp.exp(value - top)
                scaled[at, strip] = term
                new.append((total + fold(term), count + fold(jnp.where(value > SAFE, 1.0, 0.0))))
            return new

        sums = block_of(c, [(blank, blank)] * len(strips), terms)
        flat = [jnp.sum(value, axis=0, keepdims=True) for k in range(2) for value in [pair[k] for pair in sums]]
        gains[c] = jnp.concatenate(tops + flat, axis=1)

    @pl.loop(0, CHUNKS + 1)
    def _(slot):
        @pl.when(slot < CHUNKS)
        def _():
            complete(slot)

        @pl.when(slot > 0)
        def _():
            first_columns(slot - 1)

    parts = gains[...]
    local_top = jnp.max(parts[:, :, :cols], axis=0)
    local_sum = jnp.sum(parts[:, :, cols:2 * cols] * jnp.exp(parts[:, :, :cols] - local_top), axis=0)
    own_count = jnp.sum(parts[:, :, 2 * cols:], axis=0)
    col_held = own_count > 0.0
    col_first[REACH] = jnp.concatenate([local_top, local_sum, own_count], axis=1)
    near_start(col_first, tea_peer, col_phase(0))

    @pl.loop(0, CHUNKS)
    def _(c):
        near_all(row_first.at[c], stu_peer, c).wait_send()
        core_copy(c).wait_send()
        sent(c)

    near_all(col_first, tea_peer, col_phase(0)).wait_recv()
    col_pot, col_count = merge(col_first[...], cols)
    col_pot = jnp.where(col_held, col_pot, 0.0)
    for c in range(CHUNKS):
        gains[c, :, :cols] = jnp.exp(gains[c, :, :cols] + col_pot)

    def by_chunk_block(body, init=None):
        def step(b, carry):
            at = pl.ds(pl.multiple_of(b * ROW_BLOCK, ROW_BLOCK), ROW_BLOCK)
            return body(at, gains.at[b // (chunk // ROW_BLOCK)], carry)
        return lax.fori_loop(0, blocks, step, init)

    def across(pick):
        return jnp.concatenate([pick(c) for c in range(CHUNKS)], axis=1)

    row_held = across(held_rows)
    first_pot = across(lambda c: row_pots[c, :, :chunk])
    row_count = across(lambda c: row_pots[c, :, chunk:])

    for step in range(1, ITERS):
        last = step == ITERS - 1
        row_slots, col_slots = row_next.at[step - 1], col_next.at[step - 1]

        def later_rows(at, gain, carry):
            total = scaled[at, strips[0]] * gain[:, strips[0]]
            for strip in strips[1:]:
                total += scaled[at, strip] * gain[:, strip]
            right[at, :] = total
            return carry

        by_chunk_block(later_rows)
        row_slots[REACH] = to_lanes(right[...], jnp.sum)
        near_start(row_slots, stu_peer, row_phase(step))
        near_all(row_slots, stu_peer, row_phase(step)).wait_recv()
        factor = row_count / jnp.sum(row_slots[...], axis=0)
        left[...] = to_rows(jnp.where(row_held, factor, 0.0))

        def later_cols(at, gain, sums):
            factor = left[at, :]
            return [
                value + fold(scaled[at, strip] * factor) * gain[:, strip] for strip, value in zip(strips, sums)
            ]

        sums = by_chunk_block(later_cols, [blank] * len(strips))
        total = jnp.concatenate([jnp.sum(value, axis=0, keepdims=True) for value in sums], axis=1)
        if last:
            base = jnp.where(col_held, -col_pot - jnp.log(col_count), SAFE)
            col_last[place] = jnp.concatenate([base, total], axis=1)
            for k in (-2, 2, -1, 1):
                spread_copy(col_last.at[place], tea_peer, col_phase(step), k, near_send, near_recv).start()

            others = peers - 1 - 2 * REACH

            @pl.loop(0, others)
            def _(k):
                step_away = REACH + 1 + lax.rem(k + others // 2, others)
                spread_copy(col_last.at[place], tea_peer, 1, step_away).start()

            row_last[stu] = jnp.where(row_held, first_pot + jnp.log(factor), FLOOR)

            @pl.loop(1, peers)
            def _(k):
                spread_copy(row_last.at[stu], stu_peer, 0, k).start()

            near_cols = spread_copy(
                col_last.at[pl.ds(0, 2 * REACH)], tea_peer, col_phase(step), 1, near_send, near_recv
            )
            near_cols.wait_recv()
            for k in (-2, -1, 1, 2):
                total += col_last[lax.rem(place + k + peers, peers), :, cols:]
        else:
            col_slots[REACH] = total
            near_start(col_slots, tea_peer, col_phase(step))
            near_all(col_slots, tea_peer, col_phase(step)).wait_recv()
            total = jnp.sum(col_slots[...], axis=0)
        fresh = jnp.where(col_held, col_count / total, 1.0)
        col_pot = col_pot + jnp.log(fresh)
        for c in range(CHUNKS):
            gains[c, :, :cols] = gains[c, :, :cols] * fresh

    def finish(at, gain, carry):
        factor = left[at, :]
        for strip in strips:
            plan_ref[at, strip] = (scaled[at, strip] * factor * gain[:, strip]).astype(jnp.bfloat16)
        return carry

    by_chunk_block(finish)
    far_rows = spread_copy(row_last.at[pl.ds(0, peers - 1)], stu_peer, 0, 1)
    far_cols = spread_copy(col_last.at[pl.ds(0, peers - 1 - 2 * REACH)], tea_peer, 1, 1)
    near_cols.wait_send()
    near_all(col_first, tea_peer, col_phase(0)).wait_send()
    for step in range(1, ITERS):
        near_all(row_next.at[step - 1], stu_peer, row_phase(step)).wait_send()
    for step in range(1, ITERS - 1):
        near_all(col_next.at[step - 1], tea_peer, col_phase(step)).wait_send()
    far_rows.wait_recv()
    row_out[...] = jnp.max(row_last[...], axis=0).reshape(rows)
    far_cols.wait_recv()
    base, total = col_last[:, :, :cols], col_last[:, :, cols:]
    top = jnp.max(base, axis=0)
    col_out[...] = -(top + jnp.log(jnp.sum(total * jnp.exp(base - top), axis=0))).reshape(cols)

    far_rows.wait_send()
    far_cols.wait_send()

def hand_over_kernel(plan_ref, row_ref, col_ref, plan_out, row_out, col_out, sems):
    copies = [
        pltpu.make_async_copy(source, target, sems.at[k])
        for k, (source, target) in enumerate(((plan_ref, plan_out), (row_ref, row_out), (col_ref, col_out)))
    ]
    for copy in copies:
        copy.start()
    for copy in copies:
        copy.wait()


def hand_over(*held):
    anywhere = pl.BlockSpec(memory_space=pl.ANY)
    return pl.pallas_call(
        hand_over_kernel,
        out_shape=tuple(jax.ShapeDtypeStruct(value.shape, value.dtype) for value in held),
        in_specs=[pl.BlockSpec(memory_space=pltpu.VMEM)] * len(held),
        out_specs=(anywhere,) * len(held),
        scratch_shapes=[pltpu.SemaphoreType.DMA((len(held),))],
    )(*(pltpu.with_memory_space_constraint(value, pltpu.VMEM) for value in held))


def per_device(peers, teacher_hidden, projection, student_hidden, teacher_segment, student_segment):
    rows, cols, feats = teacher_segment.shape[0], student_segment.shape[0], projection.shape[0]
    depth = teacher_hidden.shape[1]
    chunk = rows // CHUNKS
    vmem = pl.BlockSpec(memory_space=pltpu.VMEM)
    anywhere = pl.BlockSpec(memory_space=pl.ANY)
    plan, row_pot, col_pot = pl.pallas_call(
        functools.partial(kernel, peers),
        out_shape=(
            pltpu.VMEM((rows, cols), jnp.bfloat16),
            pltpu.VMEM((rows,), jnp.float32),
            pltpu.VMEM((cols,), jnp.float32),
        ),
        in_specs=[anywhere] * 3 + [vmem] * 2,
        out_specs=(vmem, vmem, vmem),
        scratch_shapes=[
            pltpu.VMEM((2 * CHUNKS, chunk, depth), jnp.bfloat16),
            pltpu.VMEM((feats, depth), jnp.bfloat16),
            pltpu.VMEM((RING, cols, RING * feats), jnp.bfloat16),
            pltpu.VMEM((CHUNKS, chunk, feats), jnp.float32),
            pltpu.VMEM((2, chunk, feats), jnp.float32),
            pltpu.VMEM((CHUNKS, chunk, feats), jnp.float32),
            pltpu.VMEM((CHUNKS, RING, chunk, RING * feats), jnp.bfloat16),
            pltpu.VMEM((rows, LANES), jnp.float32),
            pltpu.VMEM((rows, LANES), jnp.float32),
            pltpu.VMEM((1, cols), jnp.float32),
            pltpu.VMEM((rows, cols), jnp.float32),
            pltpu.VMEM((rows, LANES), jnp.float32),
            pltpu.VMEM((rows, LANES), jnp.float32),
            pltpu.VMEM((rows, LANES), jnp.float32),
            pltpu.VMEM((CHUNKS, 1, 3 * cols), jnp.float32),
            pltpu.VMEM((CHUNKS, 1, 2 * chunk), jnp.float32),
            pltpu.VMEM((CHUNKS, 2 * REACH + 1, 1, 3 * chunk), jnp.float32),
            pltpu.VMEM((ITERS - 1, 2 * REACH + 1, 1, rows), jnp.float32),
            pltpu.VMEM((peers, 1, rows), jnp.float32),
            pltpu.VMEM((2 * REACH + 1, 1, 3 * cols), jnp.float32),
            pltpu.VMEM((ITERS - 1, 2 * REACH + 1, 1, cols), jnp.float32),
            pltpu.VMEM((peers, 1, 2 * cols), jnp.float32),
            pltpu.SemaphoreType.DMA((2 * CHUNKS,)),
            pltpu.SemaphoreType.DMA((2,)),
            pltpu.SemaphoreType.DMA((CHUNKS,)),
            pltpu.SemaphoreType.DMA((CHUNKS,)),
            pltpu.SemaphoreType.DMA((CHUNKS, 14)),
            pltpu.SemaphoreType.DMA((CHUNKS, 14)),
            pltpu.SemaphoreType.DMA((CHUNKS + 2 * ITERS - 1,)),
            pltpu.SemaphoreType.DMA((CHUNKS + 2 * ITERS - 1,)),
            pltpu.SemaphoreType.DMA((2,)),
            pltpu.SemaphoreType.DMA((2,)),
            pltpu.SemaphoreType.REGULAR((TEA_HALF - 1,)),
        ],
        compiler_params=pltpu.CompilerParams(
            collective_id=1, has_side_effects=True, vmem_limit_bytes=60 * 1024 * 1024
        ),
    )(teacher_hidden, projection, student_hidden, teacher_segment, student_segment)
    return hand_over(plan, row_pot, col_pot)


def solution(mesh):
    placed = (P("tea", "hid"), P("stu", "hid"), P("stu", None), P(("tea", "hid")), P("stu"))
    return jax.shard_map(
        functools.partial(per_device, mesh.shape["stu"]),
        mesh=mesh,
        in_specs=placed,
        out_specs=(P(("tea", "hid"), "stu"), P(("tea", "hid")), P("stu")),
        check_vma=False,
    )
```
